256 devices in a mesh: ctx: 32 (over z, x), dp: 8 (over y, core).
Axes of the slice: x: 4, y: 4, z: 8, core: 2. Of those that a mesh axis runs over, the one named last changes fastest.
Arguments:
- queries: bfloat16 [8, 8192, 1024], P('dp', 'ctx'), may hold values from -8 to 8
- keys: bfloat16 [8, 8192, 1024], P('dp', 'ctx'), may hold values from -8 to 8
- values: bfloat16 [8, 8192, 1024], P('dp', 'ctx'), may hold values from -6 to 6
- cotangent: bfloat16 [8, 8192, 2048], P('dp', 'ctx'), may hold values from -6 to 6
- proj_weight: bfloat16 [1024, 2048], P('dp'), may hold values from -0.1875 to 0.1875
- pattern: int32 [8, 8, 64, 2], P('dp'), may hold values 0 or 1
Outputs:
- projected: bfloat16 [8, 8192, 2048], P('dp', 'ctx')
- grad_query: bfloat16 [8, 8192, 1024], P('dp', 'ctx')
- grad_key: bfloat16 [8, 8192, 1024], P('dp', 'ctx')
- grad_value: bfloat16 [8, 8192, 1024], P('dp', 'ctx')
- grad_proj: float32 [1024, 2048], P('dp', 'ctx')
The draws below stay inside these ranges and needn't reach their ends.
Inputs may be any that keep to these rules, and one draw needn't show every extreme that they name: `pattern`: entries with o = 0 or with q - o < 1 are not read.
All inputs are finite; a program needn't handle non-finite values. No bound on the sum of `pattern` on one device may be relied on, other than what follows from the above.
Results may differ from the reference program's by a relative error of at most 0.0085.
The reference program's roundings to bfloat16 on the way count: a program that leaves them out, or rounds other values in their place, can miss the bound.
Values may be sent and summed in bfloat16 or wider, within the bound.
A program may use at most 128 MiB of HBM per device.

```python
import jax
import jax.numpy as jnp
from jax import lax

WIDTH = 2048
HEADS = 8
HDIM = 128
BLK = 128
TOK_DEV = 256
HW = 1024
BLK_DEV = 2
WIN = 2
SEQ = 8192
NQB = 64
DOCS = 8
N_CTX = 32


def query_key_pair(key):
    shape = (DOCS, SEQ, HEADS * HDIM)
    base_query = jax.random.normal(jax.random.fold_in(key, 101), shape, jnp.float32)
    base_key = jax.random.normal(jax.random.fold_in(key, 202), shape, jnp.float32)
    return (jnp.clip(base_query, -8.0, 8.0), jnp.clip(base_key, -8.0, 8.0))


def draw_queries(key, part):
    return query_key_pair(key)[0].astype(jnp.bfloat16)


def draw_keys(key, part):
    return query_key_pair(key)[1].astype(jnp.bfloat16)


def plant(result, own_key, least, top_value):
    longest = result.shape.index(max(result.shape))
    spots = []
    for shift in (0, 1):
        where = [jax.random.randint(jax.random.fold_in(own_key, axis), (), 0, length) for axis, length in enumerate(result.shape)]
        where[longest] = (where[longest] + shift) % result.shape[longest]
        spots.append(tuple(where))
    return result.at[spots[0]].set(least).at[spots[1]].set(top_value)


def spiked(array, own_key, source, target, shards_of, factor):
    def block_of(dim):
        return (jnp.arange(array.shape[dim]) // (array.shape[dim] // shards_of)).reshape((-1,) + (1,) * (array.ndim - 1 - dim))

    near = jax.random.permutation(own_key, shards_of)[block_of(target)]
    second = (block_of(target) + shards_of // 2) % shards_of
    return jnp.where((block_of(source) == near) | (block_of(source) == second), factor * array, array)


def level_of(rng, extent, split, smallest, high):
    def one(axis_at, shards_of):
        steps = jax.random.uniform(jax.random.fold_in(jax.random.fold_in(rng, 6), axis_at), (shards_of,), jnp.float32, smallest / len(split), high / len(split))
        return jnp.repeat(jnp.exp(steps), extent[axis_at] // shards_of).reshape((-1,) + (1,) * (len(extent) - axis_at - 1))

    loudness = one(*split[0])
    for cut in split[1:]:
        loudness = loudness * one(*cut)
    return loudness


def normal_values(rng, shape, deviation, bound, cuts=(), kind=jnp.bfloat16):
    drawn = deviation * jax.random.normal(rng, shape, jnp.float32)
    if cuts:
        drawn = drawn * level_of(rng, shape, cuts, -0.22, 0.18)
    return jnp.clip(drawn, -bound, bound).astype(kind)


def bell_draw_with(stream_key, shape, spread, bound, shards, heavy, held_as=jnp.bfloat16):
    drawn = spread * jax.random.normal(stream_key, shape, jnp.float32)
    if shards:
        drawn = drawn * level_of(stream_key, shape, shards, -0.22, 0.18)
    return jnp.clip(spiked(drawn, jax.random.fold_in(stream_key, 3), *heavy), -bound, bound).astype(held_as)


def setup_inputs(seed: int = 0) -> dict:
    splits = jax.random.split(jax.random.key(seed), 7)
    return {
        "queries": draw_queries(jax.random.fold_in(splits[6], 71), 0),
        "keys": draw_keys(jax.random.fold_in(splits[6], 71), 0),
        "values": normal_values(splits[2], (DOCS, SEQ, HW), 1.0, 6.0, ((0, 8), (1, 32))),
        "cotangent": bell_draw_with(splits[3], (DOCS, SEQ, WIDTH), 1.0, 6.0, ((0, 8), (1, 32)), (1, 2, 32, 2.75)),
        "proj_weight": normal_values(splits[4], (HW, WIDTH), HW ** -0.5, 0.1875, ((0, 8),)),
        "pattern": plant((jax.random.randint(splits[5], (DOCS, HEADS, NQB, WIN), 0, 2) < 1).astype(jnp.int32), jax.random.fold_in(splits[5], 1), 0, 1),
    }


masked_value = -1.0e30


def product(form, left, right):
    return jnp.einsum(form, left.astype(jnp.float32), right.astype(jnp.float32))


def block_masks(pattern_rows, query_blocks):
    column = jnp.arange(WIN * BLK, dtype=jnp.int32)
    within = jnp.arange(BLK, dtype=jnp.int32)
    offsets = WIN - 1 - jnp.arange(WIN, dtype=jnp.int32)
    flipped = jnp.flip(pattern_rows, axis=2) == 1
    key_blocks = query_blocks[:, None] - offsets[None, :]
    permitted = (flipped | (offsets == 0)[None, None, :]) & (key_blocks >= 1)[:, None, :]
    expanded = jnp.repeat(permitted, BLK, axis=2)
    causal = (column[None, :] < (WIN - 1) * BLK) | (column[None, :] - (WIN - 1) * BLK <= within[:, None])
    key_mask = expanded[:, :, None, :] & causal[None, None, :, :]
    sink_mask = (query_blocks[:, None, None] > 0) | (within[None, None, :] <= within[None, :, None])
    return key_mask, sink_mask[:, None, :, :]


def attend_scores(queries_b, key_window, sink_keys, key_mask, sink_mask, product):
    inverse_root = HDIM ** -0.5
    scores = product('nqhd,nkhd->nhqk', queries_b, key_window) * inverse_root
    sink_scores = product('nqhd,khd->nhqk', queries_b, sink_keys) * inverse_root
    return jnp.where(key_mask, scores, masked_value), jnp.where(sink_mask, sink_scores, masked_value)


def forward_blocks(queries_b, key_window, value_window, sink_keys, sink_values, key_mask, sink_mask, product):
    scores, sink_scores = attend_scores(queries_b, key_window, sink_keys, key_mask, sink_mask, product)
    row_max = jnp.maximum(jnp.max(scores, axis=-1), jnp.max(sink_scores, axis=-1))
    row_total = jnp.sum(jnp.exp(scores - row_max[..., None]), axis=-1) + jnp.sum(jnp.exp(sink_scores - row_max[..., None]), axis=-1)
    log_total = row_max + jnp.log(row_total)
    weights = jnp.exp(scores - log_total[..., None]).astype(jnp.bfloat16)
    sink_weights = jnp.exp(sink_scores - log_total[..., None]).astype(jnp.bfloat16)
    attended = product('nhqk,nkhd->nqhd', weights, value_window) + product('nhqk,khd->nqhd', sink_weights, sink_values)
    return attended.astype(jnp.bfloat16), log_total


def backward_blocks(queries_b, key_window, value_window, sink_keys, sink_values, key_mask, sink_mask, log_total, out_grad, row_delta, product):
    inverse_root = HDIM ** -0.5
    scores, sink_scores = attend_scores(queries_b, key_window, sink_keys, key_mask, sink_mask, product)
    weights = jnp.exp(scores - log_total[..., None])
    sink_weights = jnp.exp(sink_scores - log_total[..., None])
    prob_grad = product('nqhd,nkhd->nhqk', out_grad, value_window)
    sink_prob_grad = product('nqhd,khd->nhqk', out_grad, sink_values)
    score_grad = (weights * (prob_grad - row_delta[..., None])).astype(jnp.bfloat16)
    sink_score_grad = (sink_weights * (sink_prob_grad - row_delta[..., None])).astype(jnp.bfloat16)
    query_grad = inverse_root * (product('nhqk,nkhd->nqhd', score_grad, key_window) + product('nhqk,khd->nqhd', sink_score_grad, sink_keys))
    window_key_grad = inverse_root * product('nhqk,nqhd->nkhd', score_grad, queries_b)
    window_value_grad = product('nhqk,nqhd->nkhd', weights.astype(jnp.bfloat16), out_grad)
    sink_key_grad = inverse_root * product('nhqk,nqhd->khd', sink_score_grad, queries_b)
    sink_value_grad = product('nhqk,nqhd->khd', sink_weights.astype(jnp.bfloat16), out_grad)
    return query_grad, window_key_grad, window_value_grad, sink_key_grad, sink_value_grad


def make_windows(extended, first):
    pieces = [extended[(number + first) * BLK:(number + first + WIN) * BLK] for number in range(BLK_DEV)]
    return jnp.stack(pieces).reshape(BLK_DEV, WIN * BLK, HEADS, HDIM)


def place_windows(window_grad):
    flat = window_grad.reshape(BLK_DEV, WIN * BLK, HEADS * HDIM)
    placed = jnp.zeros((2 * BLK_DEV * BLK, HEADS * HDIM), jnp.float32)
    for number in range(BLK_DEV):
        placed = placed + jnp.pad(flat[number], (((number + 1) * BLK, (2 * BLK_DEV - number - 1 - WIN) * BLK), (0, 0)))
    return placed


def one_document(queries, keys, values, cotangent, pattern, proj_weight):
    width_heads = HEADS * HDIM
    zero_rows = jnp.zeros((TOK_DEV, width_heads), keys.dtype)
    key_pad = jnp.concatenate([zero_rows, keys], axis=0)
    value_pad = jnp.concatenate([zero_rows, values], axis=0)
    sink_keys = keys[:BLK].reshape(BLK, HEADS, HDIM)
    sink_values = values[:BLK].reshape(BLK, HEADS, HDIM)

    def group_inputs(group):
        start = (group * TOK_DEV).astype(jnp.int32)
        key_window = make_windows(lax.dynamic_slice_in_dim(key_pad, start, 2 * TOK_DEV, 0), 1)
        value_window = make_windows(lax.dynamic_slice_in_dim(value_pad, start, 2 * TOK_DEV, 0), 1)
        query_rows = lax.dynamic_slice_in_dim(queries, start, TOK_DEV, 0).reshape(BLK_DEV, BLK, HEADS, HDIM)
        query_blocks = (group * BLK_DEV + jnp.arange(BLK_DEV, dtype=jnp.int32)).astype(jnp.int32)
        pattern_rows = jnp.transpose(lax.dynamic_slice_in_dim(pattern, (group * BLK_DEV).astype(jnp.int32), BLK_DEV, 1), (1, 0, 2))
        key_mask, sink_mask = block_masks(pattern_rows, query_blocks)
        return query_rows, key_window, value_window, key_mask, sink_mask

    def forward_group(group):
        query_rows, key_window, value_window, key_mask, sink_mask = group_inputs(group)
        return forward_blocks(query_rows, key_window, value_window, sink_keys, sink_values, key_mask, sink_mask, product)

    groups = jnp.arange(N_CTX, dtype=jnp.int32)
    attended, log_total = lax.map(forward_group, groups)
    attended_rows = attended.reshape(SEQ, width_heads)
    projected = jnp.dot(attended_rows, proj_weight, preferred_element_type=jnp.float32).astype(jnp.bfloat16)
    grad_attended = jnp.dot(cotangent, proj_weight.T, preferred_element_type=jnp.float32).astype(jnp.bfloat16)
    weight_term = jnp.dot(attended_rows.T, cotangent, preferred_element_type=jnp.float32)
    row_delta = jnp.sum(grad_attended.astype(jnp.float32).reshape(SEQ, HEADS, HDIM) * attended_rows.astype(jnp.float32).reshape(SEQ, HEADS, HDIM), axis=-1)
    delta_groups = jnp.transpose(row_delta.reshape(N_CTX, BLK_DEV, BLK, HEADS), (0, 1, 3, 2))
    grad_groups = grad_attended.reshape(N_CTX, BLK_DEV, BLK, HEADS, HDIM)

    def backward_step(carry, inputs):
        key_acc, value_acc, sink_key_acc, sink_value_acc = carry
        group, group_lse, group_grad, group_delta = inputs
        query_rows, key_window, value_window, key_mask, sink_mask = group_inputs(group)
        query_grad, window_key, window_value, sink_key, sink_value = backward_blocks(
            query_rows, key_window, value_window, sink_keys, sink_values, key_mask, sink_mask,
            group_lse, group_grad, group_delta, product)
        start = (group * TOK_DEV).astype(jnp.int32)
        key_acc = lax.dynamic_update_slice_in_dim(key_acc, lax.dynamic_slice_in_dim(key_acc, start, 2 * TOK_DEV, 0) + place_windows(window_key), start, 0)
        value_acc = lax.dynamic_update_slice_in_dim(value_acc, lax.dynamic_slice_in_dim(value_acc, start, 2 * TOK_DEV, 0) + place_windows(window_value), start, 0)
        return (key_acc, value_acc, sink_key_acc + sink_key, sink_value_acc + sink_value), query_grad

    initial = (jnp.zeros((SEQ + TOK_DEV, width_heads), jnp.float32), jnp.zeros((SEQ + TOK_DEV, width_heads), jnp.float32),
               jnp.zeros((BLK, HEADS, HDIM), jnp.float32), jnp.zeros((BLK, HEADS, HDIM), jnp.float32))
    carry, query_grads = lax.scan(backward_step, initial, (groups, log_total, grad_groups, delta_groups))
    key_grad = carry[0][TOK_DEV:]
    value_grad = carry[1][TOK_DEV:]
    key_grad = jnp.concatenate([key_grad[:BLK] + carry[2].reshape(BLK, width_heads), key_grad[BLK:]], axis=0)
    value_grad = jnp.concatenate([value_grad[:BLK] + carry[3].reshape(BLK, width_heads), value_grad[BLK:]], axis=0)
    return (projected, query_grads.reshape(SEQ, width_heads).astype(jnp.bfloat16),
            key_grad.astype(jnp.bfloat16), value_grad.astype(jnp.bfloat16), weight_term)


def reference(queries, keys, values, cotangent, proj_weight, pattern):
    def per_document(items):
        return one_document(items[0], items[1], items[2], items[3], items[4], proj_weight)

    projected, grad_query, grad_key, grad_value, terms = lax.map(per_document, (queries, keys, values, cotangent, pattern))
    grad_proj = jnp.sum(terms, axis=0) * (DOCS * SEQ) ** -0.5
    return (projected, grad_query, grad_key, grad_value, grad_proj)
```

```python
import jax
import jax.numpy as jnp
from jax import lax
from jax.experimental import pallas as pl
from jax.experimental.pallas import tpu as pltpu
from jax.sharding import PartitionSpec as P

MESH = pl.DeviceIdType.MESH
NX, NY, NZ = 4, 4, 8
HEADS, HDIM, BLK = 8, 128, 128
BF, F32 = jnp.bfloat16, jnp.float32
MASKED = -1.0e30
UNROLL = 4
SCALE = HDIM ** -0.5
SCALE2 = SCALE * 1.4426950408889634


def lanes(index, size=128):
    return pl.ds(pl.multiple_of(index * size, size), size)


def dot(a, b, da, db):
    return lax.dot_general(a, b, (((da,), (db,)), ((), ())), preferred_element_type=F32)


def kernel(pat_ref, q_ref, k_ref, v_ref, cot_ref, w_ref,
           proj_ref, dq_ref, dk_ref, dv_ref, gp_ref,
           pat, q, cot, wfull, kv, ct, cot_peer, a2, attn_send, attn_all, grad, gate, bias, probs,
           acc, pg, pg_recv, sgk, gk1, gk1s, gk2, gk2s, gk3, sgv, gv1, gv1s, gv2, gv2s, gv3,
           ptb, xfwd, xmrg, xin, yfwd, ymrg, yin, s2x, s2y, r2x, r2y, red, r3,
           local, prev_s, prev_r, w_s, w_r, core_s, core_r, sk_s, sk_r, kz_s, kz_r, kx_s, kx_r, vz_s, vz_r,
           pg_s, pg_r, gk1_s, gk1_r, gk2_s, gk2_r, gk3_s, gk3_r, gv1_s, gv1_r, gv2_s, gv2_r, gv3_s, gv3_r,
           px_s, px_r, py_s, py_r, p2_s, p2_r, p3_s, p3_r):
    c = lax.axis_index("ctx")
    d = lax.axis_index("dp")
    x, z = lax.rem(c, NX), lax.div(c, NX)
    y, core = lax.div(d, 2), lax.rem(d, 2)

    def xpeer(o):
        return lax.rem(x + o, NX)

    def ypeer(o):
        return lax.rem(y + o, NY)

    def zpeer(o):
        return lax.rem(z + o, NZ)

    def at_x(xx):
        return (z * NX + xx, d)

    def at_z(zz):
        return (zz * NX + x, d)

    def at_y(yy):
        return (c, yy * 2 + core)

    other = 1 - core
    at_core = (c, y * 2 + other)
    has_next, has_prev = c < NX * NZ - 1, c > 0
    root, row0, col0 = c == 0, z == 0, x == 0
    pending = []

    def remote(src, dst, send, recv, device):
        return pltpu.make_async_remote_copy(src_ref=src, dst_ref=dst, send_sem=send, recv_sem=recv,
                                            device_id=device, device_id_type=MESH)

    def send(src, dst, send_sem, recv_sem, device, cond=None):
        copy = remote(src, dst, send_sem, recv_sem, device)
        pending.append((cond, copy))
        if cond is None:
            copy.start()
        else:
            pl.when(cond)(lambda: copy.start())

    def arrive(dst, recv_sem, cond=None):
        copy = remote(dst, dst, recv_sem, recv_sem, at_core)
        if cond is None:
            copy.wait_recv()
        else:
            pl.when(cond)(lambda: copy.wait_recv())

    own = pl.ds(2 * BLK, 2 * BLK)
    loads = [
        pltpu.make_async_copy(k_ref, kv.at[0, own], local.at[0]),
        pltpu.make_async_copy(v_ref, kv.at[1, own], local.at[1]),
        pltpu.make_async_copy(w_ref, wfull.at[lanes(d)], local.at[2]),
        pltpu.make_async_copy(cot_ref, cot, local.at[3]),
        pltpu.make_async_copy(q_ref, q, local.at[4]),
        pltpu.make_async_copy(pat_ref, pat, local.at[5]),
    ]
    for load in loads:
        load.start()
    sink_loads = [
        pltpu.make_async_copy(k_ref.at[pl.ds(0, BLK)], kv.at[0, pl.ds(0, BLK)], local.at[6]),
        pltpu.make_async_copy(v_ref.at[pl.ds(0, BLK)], kv.at[1, pl.ds(0, BLK)], local.at[7]),
    ]
    for load in sink_loads:
        pl.when(root)(lambda load=load: load.start())

    barrier = pltpu.get_barrier_semaphore()

    def greet(device):
        pl.semaphore_signal(barrier, inc=1, device_id=device, device_id_type=MESH)

    for o in range(1, NZ):
        greet(at_z(zpeer(o)))
    for o in range(1, NX):
        greet(at_x(xpeer(o)))
    for o in range(1, NY):
        greet(at_y(ypeer(o)))
    greet(at_core)
    far_next = (x == NX - 1) & has_next
    far_prev = col0 & has_prev
    pl.when(far_next)(lambda: greet((c + 1, d)))
    pl.when(far_prev)(lambda: greet((c - 1, d)))
    pl.semaphore_wait(barrier, NX + NY + NZ - 2 + far_next.astype(jnp.int32) + far_prev.astype(jnp.int32))

    def krows(ref, xx):
        return ref.at[pl.ds(pl.multiple_of(xx * 32, 32), 32)]

    def vrows(ref, zz):
        return ref.at[pl.ds(pl.multiple_of(zz * 16, 16), 16)]

    skeys, svalues = kv.at[0], kv.at[1]

    def kchunk(xx, zz):
        return skeys.at[pl.ds(pl.multiple_of(xx * 32, 32), 32), lanes(zz)]

    for o in (2, 1, 3):
        send(k_ref.at[pl.ds(o * 32, 32)], skeys.at[pl.ds(o * 32, 32)], sk_s.at[o], sk_r.at[0], at_x(o), root)
    for o in (4, 5, 3, 6, 2, 7, 1):
        send(v_ref.at[pl.ds(o * 16, 16)], svalues.at[pl.ds(o * 16, 16)], sk_s.at[3 + o], sk_r.at[1], at_z(o), root)

    def wrows(dd, half):
        return wfull.at[pl.ds(pl.multiple_of(dd * 128 + half * 64, 64), 64)]

    up, down, opposite = ypeer(1), ypeer(3), ypeer(2)
    for way, half in ((0, 0), (1, 1), (0, 1), (1, 0)):
        send(w_ref.at[pl.ds(half * 64, 64)], wrows(d, half), w_s.at[way, half], w_r.at[way, half], at_y((up, down)[way]))
    send(k_ref.at[pl.ds(BLK, BLK)], kv.at[0, pl.ds(BLK, BLK)], prev_s.at[0], prev_r.at[0], (c + 1, d), has_next & (z > 0))
    send(cot_ref, cot_peer, core_s.at[1], core_r.at[1], at_core)
    send(w_ref, wfull.at[lanes(d)], core_s.at[0], core_r.at[0], at_core)

    arrive(krows(skeys, x), sk_r.at[0], row0 & has_prev)
    for oz in (4, 5, 3, 6, 2, 7, 1):
        send(skeys.at[pl.ds(pl.multiple_of(x * 32, 32), 32), pl.ds(oz * 128, 128)],
             kchunk(x, oz), kz_s.at[6 + oz], sk_r.at[2], at_z(oz), row0 & has_prev)
        send(k_ref.at[pl.ds(0, 32), pl.ds(oz * 128, 128)], kchunk(0, oz), kz_s.at[13 + oz], sk_r.at[2], at_z(oz), root)
    send(k_ref.at[pl.ds(BLK, BLK)], kv.at[0, pl.ds(BLK, BLK)], prev_s.at[2], prev_r.at[0], (c + 1, d), row0)
    arrive(vrows(svalues, z), sk_r.at[1], col0 & has_prev)
    for o in (2, 1, 3):
        send(vrows(svalues, z), vrows(svalues, z), vz_s.at[6 + o], sk_r.at[3], at_x(o), col0 & has_prev)
        send(v_ref.at[pl.ds(0, 16)], svalues.at[pl.ds(0, 16)], vz_s.at[9 + o], sk_r.at[3], at_x(o), root)

    arrive(vrows(svalues, z), sk_r.at[3], x > 0)
    send(v_ref.at[pl.ds(BLK, BLK)], kv.at[1, pl.ds(BLK, BLK)], prev_s.at[1], prev_r.at[1], (c + 1, d), has_next)

    for oz in (4, 5, 3, 6, 2, 7, 1):
        send(vrows(svalues, z), vrows(svalues, z), vz_s.at[oz - 1], vz_r.at[oz - 1], at_z(zpeer(oz)),
             has_prev & ((x > 0) | (zpeer(oz) > 0)))
        send(v_ref.at[pl.ds(0, 16)], svalues.at[pl.ds(0, 16)], vz_s.at[12 + oz], vz_r.at[oz - 1], at_z(oz), root)

    arrive(kchunk(x, z), sk_r.at[2], z > 0)
    for oz in (4, 5, 3, 6, 2, 7, 1):
        send(kchunk(x, z), kchunk(x, z), kz_s.at[oz - 1], kz_r.at[oz - 1], at_z(zpeer(oz)), (zpeer(oz) > 0) & has_prev)
        send(k_ref.at[pl.ds(0, 32), pl.ds(0, 128)], kchunk(0, 0), kz_s.at[20 + oz], kz_r.at[oz - 1], at_z(oz), root)
    for load in loads:
        load.wait()
    for load in sink_loads:
        pl.when(root)(lambda load=load: load.wait())

    @pl.when(root)
    def _():
        kv[0, BLK:2 * BLK] = jnp.zeros((BLK, HEADS * HDIM), BF)
        kv[1, BLK:2 * BLK] = jnp.zeros((BLK, HEADS * HDIM), BF)

    row = lax.broadcasted_iota(jnp.int32, (2 * BLK, 4 * BLK), 0)
    col = lax.broadcasted_iota(jnp.int32, (2 * BLK, 4 * BLK), 1)
    inside = lax.rem(col, BLK) <= lax.rem(row, BLK)
    col_blk, row_blk = lax.div(col, BLK), lax.div(row, BLK)
    first_shard = jnp.full((2 * BLK, 4 * BLK), c, jnp.int32) == 0
    keep = ((col_blk == 0) & (~first_shard | (row_blk == 1) | inside)) \
        | ((col_blk == 2) & (row_blk == 0) & inside & ~first_shard) \
        | ((col_blk == 3) & (row_blk == 1) & inside) \
        | (col_blk == row_blk + 1)
    bias[...] = jnp.where(keep, 0.0, MASKED)
    reach = pat[:, 1, :]
    block = lax.broadcasted_iota(jnp.int32, reach.shape, 1)
    for n in (0, 1):
        hit = (block == 2 * c + n) & (reach == 1) & (jnp.full(reach.shape, c, jnp.int32) > 0)
        on = jnp.max(jnp.where(hit, 1.0, 0.0), axis=1, keepdims=True)
        gate[n] = jnp.zeros((HEADS, 4 * BLK), F32)
        gate[n, :, (n + 1) * BLK:(n + 2) * BLK] = jnp.broadcast_to(jnp.where(on > 0.5, 0.0, MASKED), (HEADS, BLK))

    d_down, d_up, d_opp = down * 2 + core, up * 2 + core, opposite * 2 + core
    arrive(wrows(d_down, 0), w_r.at[0, 0])
    send(wrows(d_down, 0), wrows(d_down, 0), w_s.at[2, 0], w_r.at[2, 0], at_y(up))
    arrive(wrows(d_up, 1), w_r.at[1, 1])
    send(wrows(d_up, 1), wrows(d_up, 1), w_s.at[2, 1], w_r.at[2, 1], at_y(down))

    for oz in range(1, NZ):
        arrive(kchunk(x, zpeer(NZ - oz)), kz_r.at[oz - 1], z > 0)
    for o in (2, 1, 3):
        send(krows(skeys, x), krows(skeys, x), kx_s.at[o - 1], kx_r.at[o - 1], at_x(xpeer(o)), has_prev & ((z > 0) | (xpeer(o) > 0)))
        send(k_ref.at[pl.ds(0, 32)], skeys.at[pl.ds(0, 32)], kx_s.at[2 + o], kx_r.at[o - 1], at_x(o), root)

    def turn(n, carry):
        ct[lanes(n, 256), 0:256] = cot[:, lanes(n, 256)].T
        return carry

    lax.fori_loop(0, 8, turn, 0)

    arrive(wrows(d_down, 1), w_r.at[0, 1])
    send(wfull.at[lanes(d_down)], wfull.at[lanes(d_down)], core_s.at[2], core_r.at[2], at_core)
    arrive(wrows(d_up, 0), w_r.at[1, 0])
    send(wfull.at[lanes(d_up)], wfull.at[lanes(d_up)], core_s.at[3], core_r.at[3], at_core)

    arrive(cot_peer, core_r.at[1])

    def turn_peer(n, carry):
        ct[lanes(n, 256), 256:512] = cot_peer[:, lanes(n, 256)].T
        return carry

    lax.fori_loop(0, 8, turn_peer, 0)

    for o in range(1, NX):
        arrive(krows(skeys, xpeer(NX - o)), kx_r.at[o - 1], has_prev)
    for oz in range(1, NZ):
        arrive(vrows(svalues, zpeer(NZ - oz)), vz_r.at[oz - 1], has_prev)
    arrive(kv.at[0, pl.ds(BLK, BLK)], prev_r.at[0], has_prev)
    arrive(kv.at[1, pl.ds(BLK, BLK)], prev_r.at[1], has_prev)

    def forward(h):
        cols = lanes(h)
        s = dot(q[:, cols], kv[0, :, cols], 1, 1) * SCALE2 + bias[...]
        s = jnp.concatenate([s[0:BLK] + gate[0, pl.ds(h, 1), :], s[BLK:] + gate[1, pl.ds(h, 1), :]], axis=0)
        e = jnp.exp2(s - jnp.max(s, axis=1, keepdims=True))
        p = e * (1.0 / jnp.sum(e, axis=1, keepdims=True))
        return p, dot(p.astype(BF), kv[1, :, cols], 1, 0).astype(BF)

    def forward_some(j, parity):
        heads = [2 * (UNROLL * j + n) + parity for n in range(UNROLL)]
        done = [forward(h) for h in heads]
        for n, (p, out) in enumerate(done):
            probs[heads[n]] = p
            attn_all[:, lanes(heads[n])] = out
        return [(lanes(UNROLL * j + n), out) for n, (_, out) in enumerate(done)]

    def forward_other(j, carry):
        for place, out in forward_some(j, other):
            attn_send[:, place] = out
        return carry

    def forward_own(j, carry):
        for place, out in forward_some(j, core):
            a2[0:256, place] = out
        return carry

    lax.fori_loop(0, 4 // UNROLL, forward_other, 0)
    send(attn_send, a2.at[pl.ds(256, 256)], core_s.at[4], core_r.at[4], at_core)
    arrive(wrows(d_opp, 0), w_r.at[2, 0])
    arrive(wrows(d_opp, 1), w_r.at[2, 1])
    send(wfull.at[lanes(d_opp)], wfull.at[lanes(d_opp)], core_s.at[5], core_r.at[5], at_core)
    lax.fori_loop(0, 4 // UNROLL, forward_own, 0)

    arrive(a2.at[pl.ds(256, 256)], core_r.at[4])

    def partial(zz, carry):
        ptb[zz] = dot(ct[lanes(zz, 256), :], a2[...], 1, 0).astype(BF).reshape(NX, 64, 512)
        return carry

    xu, xd, xo = xpeer(1), xpeer(3), xpeer(2)

    def xpart(lo, xx):
        return ptb.at[pl.ds(lo, 2), xx]

    def ypart(lo, yy):
        return ptb.at[pl.ds(lo, 2), :, :, lanes(yy)]

    lax.fori_loop(0, 4, partial, 0)
    send(xpart(0, xo), xfwd.at[0], px_s.at[0], px_r.at[0], at_x(xu))
    send(xpart(2, xo), xfwd.at[1], px_s.at[1], px_r.at[1], at_x(xd))
    send(xpart(2, xu), xin.at[2], px_s.at[2], px_r.at[2], at_x(xu))
    send(xpart(0, xd), xin.at[3], px_s.at[3], px_r.at[3], at_x(xd))
    lax.fori_loop(4, 8, partial, 0)
    send(ypart(4, opposite), yfwd.at[0], py_s.at[0], py_r.at[0], at_y(up))
    send(ypart(6, opposite), yfwd.at[1], py_s.at[1], py_r.at[1], at_y(down))
    send(ypart(6, up), yin.at[2], py_s.at[2], py_r.at[2], at_y(up))
    send(ypart(4, down), yin.at[3], py_s.at[3], py_r.at[3], at_y(down))

    def peer_rows(dd):
        return wfull.at[lanes(dd)]

    arrive(peer_rows(y * 2 + other), core_r.at[0])
    arrive(peer_rows(down * 2 + other), core_r.at[2])
    arrive(peer_rows(up * 2 + other), core_r.at[3])
    arrive(peer_rows(opposite * 2 + other), core_r.at[5])

    def grad_attn(n, carry):
        grad[:, lanes(n, 256)] = dot(cot[...], wfull[lanes(n, 256), :], 1, 1).astype(BF)
        return carry

    lax.fori_loop(0, 4, grad_attn, 0)

    def backward_values(j, carry):
        places = [lanes(UNROLL * j + n) for n in range(UNROLL)]
        terms = [dot(probs[UNROLL * j + n].astype(BF), grad[:, cols], 0, 0) for n, cols in enumerate(places)]
        for cols, term in zip(places, terms):
            sgv[:, cols] = term[0:128].astype(BF)
            pg[1, :, cols] = term[128:256].astype(BF)
            acc[1, :, cols] = term[256:512]
        return carry

    lax.fori_loop(0, HEADS // UNROLL, backward_values, 0)
    for oz in (4, 5, 3, 6, 2, 7, 1):
        send(vrows(sgv, zpeer(oz)), gv1.at[oz - 1], gv1_s.at[oz - 1], gv1_r.at[oz - 1], at_z(zpeer(oz)))

    def merge(fwd, part):
        return (fwd.astype(F32) + part.astype(F32)).astype(BF)

    arrive(xfwd.at[0], px_r.at[0])
    xmrg[0] = merge(xfwd[0], ptb[0:2, xu])
    send(xmrg.at[0], xin.at[0], px_s.at[4], px_r.at[4], at_x(xu))
    arrive(xfwd.at[1], px_r.at[1])
    xmrg[1] = merge(xfwd[1], ptb[2:4, xd])
    send(xmrg.at[1], xin.at[1], px_s.at[5], px_r.at[5], at_x(xd))
    arrive(yfwd.at[0], py_r.at[0])
    ymrg[0] = merge(yfwd[0], ptb[4:6, :, :, lanes(up)])
    send(ymrg.at[0], yin.at[0], py_s.at[4], py_r.at[4], at_y(up))
    arrive(yfwd.at[1], py_r.at[1])
    ymrg[1] = merge(yfwd[1], ptb[6:8, :, :, lanes(down)])
    send(ymrg.at[1], yin.at[1], py_s.at[5], py_r.at[5], at_y(down))
    send(pg.at[1], pg_recv.at[1], pg_s.at[1], pg_r.at[1], (c - 1, d), has_prev)

    def backward_head(h):
        cols = lanes(h)
        g = grad[:, cols]
        delta = jnp.sum(g.astype(F32) * attn_all[:, cols].astype(F32), axis=1, keepdims=True)
        ds = (probs[h] * (dot(g, kv[1, :, cols], 1, 1) - delta)).astype(BF)
        return cols, dot(ds, q[:, cols], 0, 0) * SCALE, (dot(ds, kv[0, :, cols], 1, 0) * SCALE).astype(BF)

    def backward(j, carry):
        for cols, term, query_grad in [backward_head(UNROLL * j + n) for n in range(UNROLL)]:
            sgk[:, cols] = term[0:128].astype(BF)
            pg[0, :, cols] = term[128:256].astype(BF)
            acc[0, :, cols] = term[256:512]
            dq_ref[:, cols] = query_grad
        return carry

    lax.fori_loop(0, HEADS // UNROLL, backward, 0)
    for o in (2, 1, 3):
        send(krows(sgk, xpeer(o)), gk1.at[o - 1], gk1_s.at[o - 1], gk1_r.at[o - 1], at_x(xpeer(o)))

    for oz in range(1, NZ):
        arrive(gv1.at[oz - 1], gv1_r.at[oz - 1])
    total = sgv[pl.ds(pl.multiple_of(z * 16, 16), 16), :].astype(F32)
    for oz in range(1, NZ):
        total += gv1[oz - 1].astype(F32)
    gv1s[...] = total.astype(BF)
    send(gv1s, gv2.at[x], gv2_s, gv2_r.at[x], at_x(0), x > 0)

    arrive(xin.at[0], px_r.at[4])
    arrive(xin.at[3], px_r.at[3])
    arrive(xin.at[1], px_r.at[5])
    arrive(xin.at[2], px_r.at[2])
    for half in (0, 1):
        both = slice(2 * half, 2 * half + 2)
        s2x[both] = (ptb[both, x].astype(F32) + xin[half].astype(F32) + xin[3 - half].astype(F32)).astype(BF)
    for o in (2, 1, 3):
        send(s2x.at[:, :, lanes(ypeer(o))], r2y.at[o - 1], p2_s.at[o - 1], p2_r.at[o - 1], at_y(ypeer(o)))
    arrive(yin.at[0], py_r.at[4])
    arrive(yin.at[3], py_r.at[3])
    arrive(yin.at[1], py_r.at[5])
    arrive(yin.at[2], py_r.at[2])
    for half in (0, 1):
        both, here = slice(4 + 2 * half, 6 + 2 * half), slice(2 * half, 2 * half + 2)
        s2y[here] = (ptb[both, :, :, lanes(y)].astype(F32) + yin[half].astype(F32) + yin[3 - half].astype(F32)).astype(BF)
    for o in (2, 1, 3):
        send(s2y.at[:, xpeer(o)], r2x.at[o - 1], p2_s.at[o + 2], p2_r.at[o + 2], at_x(xpeer(o)))

    for o in range(1, NX):
        arrive(gk1.at[o - 1], gk1_r.at[o - 1])
    total = sgk[pl.ds(pl.multiple_of(x * 32, 32), 32), :].astype(F32)
    for o in range(1, NX):
        total += gk1[o - 1].astype(F32)
    gk1s[...] = total.astype(BF)
    send(gk1s, gk2.at[z], gk2_s, gk2_r.at[z], at_z(0), z > 0)

    @pl.when(col0)
    def _():
        for xx in range(1, NX):
            arrive(gv2.at[xx], gv2_r.at[xx])
        total = gv1s[...].astype(F32)
        for xx in range(1, NX):
            total += gv2[xx].astype(F32)
        gv2s[...] = total.astype(BF)

    send(gv2s, gv3.at[z], gv3_s, gv3_r.at[z], at_z(0), col0 & has_prev)

    def project(n, carry):
        proj_ref[:, lanes(n, 256)] = dot(attn_all[...], wfull[:, lanes(n, 256)], 1, 0).astype(BF)
        return carry

    lax.fori_loop(0, 4, project, 0)

    for o in range(1, NX):
        arrive(r2y.at[o - 1], p2_r.at[o - 1])
    total = s2x[:, :, lanes(y)].astype(F32)
    for o in range(1, NY):
        total += r2y[o - 1].astype(F32)
    red[0:4] = total.astype(BF)
    for o in range(1, NX):
        arrive(r2x.at[o - 1], p2_r.at[o + 2])
    total = s2y[:, x].astype(F32)
    for o in range(1, NX):
        total += r2x[o - 1].astype(F32)
    red[4:8] = total.astype(BF)
    for oz in (4, 5, 3, 6, 2, 7, 1):
        send(red.at[zpeer(oz)], r3.at[oz - 1], p3_s.at[oz - 1], p3_r.at[oz - 1], at_z(zpeer(oz)))
    send(pg.at[0], pg_recv.at[0], pg_s.at[0], pg_r.at[0], (c - 1, d), has_prev)

    @pl.when(row0)
    def _():
        for zz in range(1, NZ):
            arrive(gk2.at[zz], gk2_r.at[zz])
        total = gk1s[...].astype(F32)
        for zz in range(1, NZ):
            total += gk2[zz].astype(F32)
        gk2s[...] = total.astype(BF)

    send(gk2s, gk3.at[x], gk3_s, gk3_r.at[x], at_x(0), row0 & has_prev)

    lax.fori_loop(4, 8, project, 0)

    for n, out_ref in ((1, dv_ref), (0, dk_ref)):
        arrive(pg_recv.at[n], pg_r.at[n], has_next)
        out_ref[0:BLK] = acc[n, 0:BLK].astype(BF)

        @pl.when(has_next)
        def _(n=n, out_ref=out_ref):
            out_ref[BLK:] = (acc[n, BLK:] + pg_recv[n].astype(F32)).astype(BF)

        @pl.when(jnp.logical_not(has_next))
        def _(n=n, out_ref=out_ref):
            out_ref[BLK:] = acc[n, BLK:].astype(BF)

    for oz in range(1, NZ):
        arrive(r3.at[oz - 1], p3_r.at[oz - 1])
    total = red[z].astype(F32)
    for oz in range(1, NZ):
        total += r3[oz - 1].astype(F32)
    gp_ref[...] = total * (1.0 / 256.0)

    @pl.when(root)
    def _():
        for zz in range(1, NZ):
            arrive(gv3.at[zz], gv3_r.at[zz])
        for zz in range(NZ):
            rows = slice(16 * zz, 16 * zz + 16)
            part = gv2s[...] if zz == 0 else gv3[zz]
            dv_ref[rows] = (acc[1, rows] + part.astype(F32)).astype(BF)
        for xx in range(1, NX):
            arrive(gk3.at[xx], gk3_r.at[xx])
        for xx in range(NX):
            rows = slice(32 * xx, 32 * xx + 32)
            part = gk2s[...] if xx == 0 else gk3[xx]
            dk_ref[rows] = (acc[0, rows] + part.astype(F32)).astype(BF)

    for cond, copy in pending:
        if cond is None:
            copy.wait_send()
        else:
            pl.when(cond)(lambda copy=copy: copy.wait_send())


def store(*refs):
    count = (len(refs) - 1) // 2
    copies = [pltpu.make_async_copy(refs[n], refs[count + n], refs[-1].at[n]) for n in range(count)]
    for copy in copies:
        copy.start()
    for copy in copies:
        copy.wait()


def body(queries, keys, values, cotangent, proj_weight, pattern):
    rows, width = queries.shape[1:]
    full = cotangent.shape[2]
    vmem, hbm = pl.BlockSpec(memory_space=pltpu.VMEM), pl.BlockSpec(memory_space=pltpu.HBM)
    V, D = pltpu.VMEM, pltpu.SemaphoreType.DMA
    scratch = [
        V((HEADS, 2, 64), jnp.int32), V((rows, width), BF), V((rows, full), BF),
        V((1024, full), BF), V((2, 512, width), BF), V((full, 512), BF), V((rows, full), BF),
        V((512, 512), BF), V((rows, 512), BF), V((rows, width), BF), V((rows, width), BF),
        V((2, HEADS, 4 * BLK), F32), V((256, 512), F32), V((HEADS, 256, 512), F32),
        V((2, 256, width), F32), V((2, 128, width), BF), V((2, 128, width), BF),
        V((128, width), BF), V((3, 32, width), BF), V((32, width), BF), V((8, 32, width), BF), V((32, width), BF), V((4, 32, width), BF),
        V((128, width), BF), V((7, 16, width), BF), V((16, width), BF), V((4, 16, width), BF), V((16, width), BF), V((8, 16, width), BF),
        V((8, 4, 64, 512), BF),
        V((2, 2, 64, 512), BF), V((2, 2, 64, 512), BF), V((4, 2, 64, 512), BF),
        V((2, 2, 4, 64, 128), BF), V((2, 2, 4, 64, 128), BF), V((4, 2, 4, 64, 128), BF),
        V((4, 64, 512), BF), V((4, 4, 64, 128), BF), V((3, 4, 64, 128), BF), V((3, 4, 64, 128), BF),
        V((8, 64, 128), BF), V((7, 64, 128), BF),
        D((8,)), D((3,)), D((2,)), D((3, 2)), D((3, 2)), D((6,)), D((6,)), D((11,)), D((4,)), D((28,)), D((7,)), D((6,)), D((3,)),
        D((20,)), D((7,)),
        D((2,)), D((2,)), D((3,)), D((3,)), D, D((8,)), D, D((4,)), D((7,)), D((7,)), D, D((4,)), D, D((8,)),
        D((6,)), D((6,)), D((6,)), D((6,)), D((6,)), D((6,)), D((7,)), D((7,)),
    ]
    shapes = [((rows, full), BF), ((rows, width), BF), ((rows, width), BF), ((rows, width), BF), ((64, 128), F32)]
    outs = pl.pallas_call(
        kernel,
        out_shape=[pltpu.VMEM(*s) for s in shapes],
        in_specs=[hbm] * 6,
        out_specs=[vmem] * 5,
        scratch_shapes=scratch,
        compiler_params=pltpu.CompilerParams(
            collective_id=0, has_side_effects=True, vmem_limit_bytes=58 * 1024 * 1024
        ),
        cost_estimate=pl.CostEstimate(flops=4_400_000_000, bytes_accessed=6_500_000, transcendentals=1_000_000),
    )(jnp.swapaxes(pattern, 2, 3)[0], queries[0], keys[0], values[0], cotangent[0], proj_weight)
    proj, dq, dk, dv, gp = pl.pallas_call(
        store,
        out_shape=[jax.ShapeDtypeStruct(*s) for s in shapes],
        in_specs=[pl.BlockSpec(memory_space=pl.ANY)] * 5,
        out_specs=[hbm] * 5,
        scratch_shapes=[D((5,))],
        compiler_params=pltpu.CompilerParams(vmem_limit_bytes=1024 * 1024),
    )(*outs)
    return proj[None], dq[None], dk[None], dv[None], gp.T


def solution(mesh):
    return jax.shard_map(
        body,
        mesh=mesh,
        in_specs=(
            P("dp", "ctx", None),
            P("dp", "ctx", None),
            P("dp", "ctx", None),
            P("dp", "ctx", None),
            P("dp", None),
            P("dp", None, None, None),
        ),
        out_specs=(
            P("dp", "ctx", None),
            P("dp", "ctx", None),
            P("dp", "ctx", None),
            P("dp", "ctx", None),
            P("dp", "ctx"),
        ),
        check_vma=False,
    )
```

```python
import jax
import jax.numpy as jnp
from jax import lax
from jax.experimental import pallas as pl
from jax.experimental.pallas import tpu as pltpu
from jax.sharding import PartitionSpec as P

MESH = pl.DeviceIdType.MESH
NX, NY, NZ = 4, 4, 8
HEADS, HDIM, BLK = 8, 128, 128
BF, F32 = jnp.bfloat16, jnp.float32
MASKED = -1.0e30
UNROLL = 4
SCALE = HDIM ** -0.5
SCALE2 = SCALE * 1.4426950408889634


def lanes(index, size=128):
    return pl.ds(pl.multiple_of(index * size, size), size)


def dot(a, b, da, db):
    return lax.dot_general(a, b, (((da,), (db,)), ((), ())), preferred_element_type=F32)


def kernel(pat_ref, q_ref, k_ref, v_ref, cot_ref, w_ref,
           proj_ref, dq_ref, dk_ref, dv_ref, gp_ref,
           pat, q, cot, wfull, kv, ct, cot_peer, a2, attn_send, attn_all, grad, gate, bias, probs,
           acc, pg, pg_recv, sgk, gk1, gk1s, gk2, gk2s, gk3, sgv, gv1, gv1s, gv2, gv2s, gv3,
           ptb, xfwd, xmrg, xin, yfwd, ymrg, yin, s2x, s2y, r2x, r2y, red, r3,
           local, prev_s, prev_r, w_s, w_r, core_s, core_r, sk_s, sk_r, kz_s, kz_r, kx_s, kx_r, vz_s, vz_r,
           pg_s, pg_r, gk1_s, gk1_r, gk2_s, gk2_r, gk3_s, gk3_r, gv1_s, gv1_r, gv2_s, gv2_r, gv3_s, gv3_r,
           px_s, px_r, py_s, py_r, p2_s, p2_r, p3_s, p3_r):
    c = lax.axis_index("ctx")
    d = lax.axis_index("dp")
    x, z = lax.rem(c, NX), lax.div(c, NX)
    y, core = lax.div(d, 2), lax.rem(d, 2)

    def xpeer(o):
        return lax.rem(x + o, NX)

    def ypeer(o):
        return lax.rem(y + o, NY)

    def zpeer(o):
        return lax.rem(z + o, NZ)

    def at_x(xx):
        return (z * NX + xx, d)

    def at_z(zz):
        return (zz * NX + x, d)

    def at_y(yy):
        return (c, yy * 2 + core)

    other = 1 - core
    at_core = (c, y * 2 + other)
    has_next, has_prev = c < NX * NZ - 1, c > 0
    root, row0, col0 = c == 0, z == 0, x == 0
    pending = []

    def remote(src, dst, send, recv, device):
        return pltpu.make_async_remote_copy(src_ref=src, dst_ref=dst, send_sem=send, recv_sem=recv,
                                            device_id=device, device_id_type=MESH)

    def send(src, dst, send_sem, recv_sem, device, cond=None):
        copy = remote(src, dst, send_sem, recv_sem, device)
        pending.append((cond, copy))
        if cond is None:
            copy.start()
        else:
            pl.when(cond)(lambda: copy.start())

    def arrive(dst, recv_sem, cond=None):
        copy = remote(dst, dst, recv_sem, recv_sem, at_core)
        if cond is None:
            copy.wait_recv()
        else:
            pl.when(cond)(lambda: copy.wait_recv())

    own = pl.ds(2 * BLK, 2 * BLK)
    loads = [
        pltpu.make_async_copy(k_ref, kv.at[0, own], local.at[0]),
        pltpu.make_async_copy(v_ref, kv.at[1, own], local.at[1]),
        pltpu.make_async_copy(w_ref, wfull.at[lanes(d)], local.at[2]),
        pltpu.make_async_copy(cot_ref, cot, local.at[3]),
        pltpu.make_async_copy(q_ref, q, local.at[4]),
        pltpu.make_async_copy(pat_ref, pat, local.at[5]),
    ]
    for load in loads:
        load.start()
    sink_loads = [
        pltpu.make_async_copy(k_ref.at[pl.ds(0, BLK)], kv.at[0, pl.ds(0, BLK)], local.at[6]),
        pltpu.make_async_copy(v_ref.at[pl.ds(0, BLK)], kv.at[1, pl.ds(0, BLK)], local.at[7]),
    ]
    for load in sink_loads:
        pl.when(root)(lambda load=load: load.start())

    barrier = pltpu.get_barrier_semaphore()

    def greet(device):
        pl.semaphore_signal(barrier, inc=1, device_id=device, device_id_type=MESH)

    for o in range(1, NZ):
        greet(at_z(zpeer(o)))
    for o in range(1, NX):
        greet(at_x(xpeer(o)))
    for o in range(1, NY):
        greet(at_y(ypeer(o)))
    greet(at_core)
    far_next = (x == NX - 1) & has_next
    far_prev = col0 & has_prev
    pl.when(far_next)(lambda: greet((c + 1, d)))
    pl.when(far_prev)(lambda: greet((c - 1, d)))
    pl.semaphore_wait(barrier, NX + NY + NZ - 2 + far_next.astype(jnp.int32) + far_prev.astype(jnp.int32))

    def krows(ref, xx):
        return ref.at[pl.ds(pl.multiple_of(xx * 32, 32), 32)]

    def vrows(ref, zz):
        return ref.at[pl.ds(pl.multiple_of(zz * 16, 16), 16)]

    skeys, svalues = kv.at[0], kv.at[1]

    def kchunk(xx, zz):
        return skeys.at[pl.ds(pl.multiple_of(xx * 32, 32), 32), lanes(zz)]

    for o in (2, 1, 3):
        send(k_ref.at[pl.ds(o * 32, 32)], skeys.at[pl.ds(o * 32, 32)], sk_s.at[o], sk_r.at[0], at_x(o), root)
    for o in (4, 5, 3, 6, 2, 7, 1):
        send(v_ref.at[pl.ds(o * 16, 16)], svalues.at[pl.ds(o * 16, 16)], sk_s.at[3 + o], sk_r.at[1], at_z(o), root)

    def wrows(dd, half):
        return wfull.at[pl.ds(pl.multiple_of(dd * 128 + half * 64, 64), 64)]

    up, down, opposite = ypeer(1), ypeer(3), ypeer(2)
    for way, half in ((0, 0), (1, 1), (0, 1), (1, 0)):
        send(w_ref.at[pl.ds(half * 64, 64)], wrows(d, half), w_s.at[way, half], w_r.at[way, half], at_y((up, down)[way]))
    send(k_ref.at[pl.ds(BLK, BLK)], kv.at[0, pl.ds(BLK, BLK)], prev_s.at[0], prev_r.at[0], (c + 1, d), has_next & (z > 0))
    send(cot_ref, cot_peer, core_s.at[1], core_r.at[1], at_core)
    send(w_ref, wfull.at[lanes(d)], core_s.at[0], core_r.at[0], at_core)

    arrive(krows(skeys, x), sk_r.at[0], row0 & has_prev)
    for oz in (4, 5, 3, 6, 2, 7, 1):
        send(skeys.at[pl.ds(pl.multiple_of(x * 32, 32), 32), pl.ds(oz * 128, 128)],
             kchunk(x, oz), kz_s.at[6 + oz], sk_r.at[2], at_z(oz), row0 & has_prev)
        send(k_ref.at[pl.ds(0, 32), pl.ds(oz * 128, 128)], kchunk(0, oz), kz_s.at[13 + oz], sk_r.at[2], at_z(oz), root)
    send(k_ref.at[pl.ds(BLK, BLK)], kv.at[0, pl.ds(BLK, BLK)], prev_s.at[2], prev_r.at[0], (c + 1, d), row0)
    arrive(kchunk(x, z), sk_r.at[2], z > 0)
    for oz in (4, 5, 3, 6, 2, 7, 1):
        send(kchunk(x, z), kchunk(x, z), kz_s.at[oz - 1], kz_r.at[oz - 1], at_z(zpeer(oz)), (zpeer(oz) > 0) & has_prev)
        send(k_ref.at[pl.ds(0, 32), pl.ds(0, 128)], kchunk(0, 0), kz_s.at[20 + oz], kz_r.at[oz - 1], at_z(oz), root)
    arrive(vrows(svalues, z), sk_r.at[1], col0 & has_prev)
    for o in (2, 1, 3):
        send(vrows(svalues, z), vrows(svalues, z), vz_s.at[6 + o], sk_r.at[3], at_x(o), col0 & has_prev)
        send(v_ref.at[pl.ds(0, 16)], svalues.at[pl.ds(0, 16)], vz_s.at[9 + o], sk_r.at[3], at_x(o), root)

    arrive(vrows(svalues, z), sk_r.at[3], x > 0)
    send(v_ref.at[pl.ds(BLK, BLK)], kv.at[1, pl.ds(BLK, BLK)], prev_s.at[1], prev_r.at[1], (c + 1, d), has_next)

    for oz in (4, 5, 3, 6, 2, 7, 1):
        send(vrows(svalues, z), vrows(svalues, z), vz_s.at[oz - 1], vz_r.at[oz - 1], at_z(zpeer(oz)),
             has_prev & ((x > 0) | (zpeer(oz) > 0)))
        send(v_ref.at[pl.ds(0, 16)], svalues.at[pl.ds(0, 16)], vz_s.at[12 + oz], vz_r.at[oz - 1], at_z(oz), root)

    for load in loads:
        load.wait()
    for load in sink_loads:
        pl.when(root)(lambda load=load: load.wait())

    @pl.when(root)
    def _():
        kv[0, BLK:2 * BLK] = jnp.zeros((BLK, HEADS * HDIM), BF)
        kv[1, BLK:2 * BLK] = jnp.zeros((BLK, HEADS * HDIM), BF)

    row = lax.broadcasted_iota(jnp.int32, (2 * BLK, 4 * BLK), 0)
    col = lax.broadcasted_iota(jnp.int32, (2 * BLK, 4 * BLK), 1)
    inside = lax.rem(col, BLK) <= lax.rem(row, BLK)
    col_blk, row_blk = lax.div(col, BLK), lax.div(row, BLK)
    first_shard = jnp.full((2 * BLK, 4 * BLK), c, jnp.int32) == 0
    keep = ((col_blk == 0) & (~first_shard | (row_blk == 1) | inside)) \
        | ((col_blk == 2) & (row_blk == 0) & inside & ~first_shard) \
        | ((col_blk == 3) & (row_blk == 1) & inside) \
        | (col_blk == row_blk + 1)
    bias[...] = jnp.where(keep, 0.0, MASKED)
    reach = pat[:, 1, :]
    block = lax.broadcasted_iota(jnp.int32, reach.shape, 1)
    for n in (0, 1):
        hit = (block == 2 * c + n) & (reach == 1) & (jnp.full(reach.shape, c, jnp.int32) > 0)
        on = jnp.max(jnp.where(hit, 1.0, 0.0), axis=1, keepdims=True)
        gate[n] = jnp.zeros((HEADS, 4 * BLK), F32)
        gate[n, :, (n + 1) * BLK:(n + 2) * BLK] = jnp.broadcast_to(jnp.where(on > 0.5, 0.0, MASKED), (HEADS, BLK))

    d_down, d_up, d_opp = down * 2 + core, up * 2 + core, opposite * 2 + core
    arrive(wrows(d_down, 0), w_r.at[0, 0])
    send(wrows(d_down, 0), wrows(d_down, 0), w_s.at[2, 0], w_r.at[2, 0], at_y(up))
    arrive(wrows(d_up, 1), w_r.at[1, 1])
    send(wrows(d_up, 1), wrows(d_up, 1), w_s.at[2, 1], w_r.at[2, 1], at_y(down))

    for oz in range(1, NZ):
        arrive(kchunk(x, zpeer(NZ - oz)), kz_r.at[oz - 1], z > 0)
    for o in (2, 1, 3):
        send(krows(skeys, x), krows(skeys, x), kx_s.at[o - 1], kx_r.at[o - 1], at_x(xpeer(o)), has_prev & ((z > 0) | (xpeer(o) > 0)))
        send(k_ref.at[pl.ds(0, 32)], skeys.at[pl.ds(0, 32)], kx_s.at[2 + o], kx_r.at[o - 1], at_x(o), root)

    def turn(n, carry):
        ct[lanes(n, 256), 0:256] = cot[:, lanes(n, 256)].T
        return carry

    lax.fori_loop(0, 8, turn, 0)

    arrive(wrows(d_down, 1), w_r.at[0, 1])
    send(wfull.at[lanes(d_down)], wfull.at[lanes(d_down)], core_s.at[2], core_r.at[2], at_core)
    arrive(wrows(d_up, 0), w_r.at[1, 0])
    send(wfull.at[lanes(d_up)], wfull.at[lanes(d_up)], core_s.at[3], core_r.at[3], at_core)

    arrive(cot_peer, core_r.at[1])

    def turn_peer(n, carry):
        ct[lanes(n, 256), 256:512] = cot_peer[:, lanes(n, 256)].T
        return carry

    lax.fori_loop(0, 8, turn_peer, 0)

    for o in range(1, NX):
        arrive(krows(skeys, xpeer(NX - o)), kx_r.at[o - 1], has_prev)
    for oz in range(1, NZ):
        arrive(vrows(svalues, zpeer(NZ - oz)), vz_r.at[oz - 1], has_prev)
    arrive(kv.at[0, pl.ds(BLK, BLK)], prev_r.at[0], has_prev)
    arrive(kv.at[1, pl.ds(BLK, BLK)], prev_r.at[1], has_prev)

    def forward(h):
        cols = lanes(h)
        s = dot(q[:, cols], kv[0, :, cols], 1, 1) * SCALE2 + bias[...]
        s = jnp.concatenate([s[0:BLK] + gate[0, pl.ds(h, 1), :], s[BLK:] + gate[1, pl.ds(h, 1), :]], axis=0)
        e = jnp.exp2(s - jnp.max(s, axis=1, keepdims=True))
        p = e * (1.0 / jnp.sum(e, axis=1, keepdims=True))
        return p, dot(p.astype(BF), kv[1, :, cols], 1, 0).astype(BF)

    def forward_some(j, parity):
        heads = [2 * (UNROLL * j + n) + parity for n in range(UNROLL)]
        done = [forward(h) for h in heads]
        for n, (p, out) in enumerate(done):
            probs[heads[n]] = p
            attn_all[:, lanes(heads[n])] = out
        return [(lanes(UNROLL * j + n), out) for n, (_, out) in enumerate(done)]

    def forward_other(j, carry):
        for place, out in forward_some(j, other):
            attn_send[:, place] = out
        return carry

    def forward_own(j, carry):
        for place, out in forward_some(j, core):
            a2[0:256, place] = out
        return carry

    lax.fori_loop(0, 4 // UNROLL, forward_other, 0)
    send(attn_send, a2.at[pl.ds(256, 256)], core_s.at[4], core_r.at[4], at_core)
    arrive(wrows(d_opp, 0), w_r.at[2, 0])
    arrive(wrows(d_opp, 1), w_r.at[2, 1])
    send(wfull.at[lanes(d_opp)], wfull.at[lanes(d_opp)], core_s.at[5], core_r.at[5], at_core)
    lax.fori_loop(0, 4 // UNROLL, forward_own, 0)

    arrive(a2.at[pl.ds(256, 256)], core_r.at[4])

    def partial(zz, carry):
        ptb[zz] = dot(ct[lanes(zz, 256), :], a2[...], 1, 0).astype(BF).reshape(NX, 64, 512)
        return carry

    xu, xd, xo = xpeer(1), xpeer(3), xpeer(2)

    def xpart(lo, xx):
        return ptb.at[pl.ds(lo, 2), xx]

    def ypart(lo, yy):
        return ptb.at[pl.ds(lo, 2), :, :, lanes(yy)]

    lax.fori_loop(0, 4, partial, 0)
    send(xpart(0, xo), xfwd.at[0], px_s.at[0], px_r.at[0], at_x(xu))
    send(xpart(2, xo), xfwd.at[1], px_s.at[1], px_r.at[1], at_x(xd))
    send(xpart(2, xu), xin.at[2], px_s.at[2], px_r.at[2], at_x(xu))
    send(xpart(0, xd), xin.at[3], px_s.at[3], px_r.at[3], at_x(xd))
    lax.fori_loop(4, 8, partial, 0)
    send(ypart(4, opposite), yfwd.at[0], py_s.at[0], py_r.at[0], at_y(up))
    send(ypart(6, opposite), yfwd.at[1], py_s.at[1], py_r.at[1], at_y(down))
    send(ypart(6, up), yin.at[2], py_s.at[2], py_r.at[2], at_y(up))
    send(ypart(4, down), yin.at[3], py_s.at[3], py_r.at[3], at_y(down))

    def peer_rows(dd):
        return wfull.at[lanes(dd)]

    arrive(peer_rows(y * 2 + other), core_r.at[0])
    arrive(peer_rows(down * 2 + other), core_r.at[2])
    arrive(peer_rows(up * 2 + other), core_r.at[3])
    arrive(peer_rows(opposite * 2 + other), core_r.at[5])

    def grad_attn(n, carry):
        grad[:, lanes(n, 256)] = dot(cot[...], wfull[lanes(n, 256), :], 1, 1).astype(BF)
        return carry

    lax.fori_loop(0, 4, grad_attn, 0)

    def backward_values(j, carry):
        places = [lanes(UNROLL * j + n) for n in range(UNROLL)]
        terms = [dot(probs[UNROLL * j + n].astype(BF), grad[:, cols], 0, 0) for n, cols in enumerate(places)]
        for cols, term in zip(places, terms):
            sgv[:, cols] = term[0:128].astype(BF)
            pg[1, :, cols] = term[128:256].astype(BF)
            acc[1, :, cols] = term[256:512]
        return carry

    lax.fori_loop(0, HEADS // UNROLL, backward_values, 0)
    for oz in (4, 5, 3, 6, 2, 7, 1):
        send(vrows(sgv, zpeer(oz)), gv1.at[oz - 1], gv1_s.at[oz - 1], gv1_r.at[oz - 1], at_z(zpeer(oz)))

    def merge(fwd, part):
        return (fwd.astype(F32) + part.astype(F32)).astype(BF)

    arrive(xfwd.at[0], px_r.at[0])
    xmrg[0] = merge(xfwd[0], ptb[0:2, xu])
    send(xmrg.at[0], xin.at[0], px_s.at[4], px_r.at[4], at_x(xu))
    arrive(xfwd.at[1], px_r.at[1])
    xmrg[1] = merge(xfwd[1], ptb[2:4, xd])
    send(xmrg.at[1], xin.at[1], px_s.at[5], px_r.at[5], at_x(xd))
    arrive(yfwd.at[0], py_r.at[0])
    ymrg[0] = merge(yfwd[0], ptb[4:6, :, :, lanes(up)])
    send(ymrg.at[0], yin.at[0], py_s.at[4], py_r.at[4], at_y(up))
    arrive(yfwd.at[1], py_r.at[1])
    ymrg[1] = merge(yfwd[1], ptb[6:8, :, :, lanes(down)])
    send(ymrg.at[1], yin.at[1], py_s.at[5], py_r.at[5], at_y(down))
    send(pg.at[1], pg_recv.at[1], pg_s.at[1], pg_r.at[1], (c - 1, d), has_prev)

    def backward_head(h):
        cols = lanes(h)
        g = grad[:, cols]
        delta = jnp.sum(g.astype(F32) * attn_all[:, cols].astype(F32), axis=1, keepdims=True)
        ds = (probs[h] * (dot(g, kv[1, :, cols], 1, 1) - delta)).astype(BF)
        return cols, dot(ds, q[:, cols], 0, 0) * SCALE, (dot(ds, kv[0, :, cols], 1, 0) * SCALE).astype(BF)

    def backward(j, carry):
        for cols, term, query_grad in [backward_head(UNROLL * j + n) for n in range(UNROLL)]:
            sgk[:, cols] = term[0:128].astype(BF)
            pg[0, :, cols] = term[128:256].astype(BF)
            acc[0, :, cols] = term[256:512]
            dq_ref[:, cols] = query_grad
        return carry

    lax.fori_loop(0, HEADS // UNROLL, backward, 0)
    for o in (2, 1, 3):
        send(krows(sgk, xpeer(o)), gk1.at[o - 1], gk1_s.at[o - 1], gk1_r.at[o - 1], at_x(xpeer(o)))

    for oz in range(1, NZ):
        arrive(gv1.at[oz - 1], gv1_r.at[oz - 1])
    total = sgv[pl.ds(pl.multiple_of(z * 16, 16), 16), :].astype(F32)
    for oz in range(1, NZ):
        total += gv1[oz - 1].astype(F32)
    gv1s[...] = total.astype(BF)
    send(gv1s, gv2.at[x], gv2_s, gv2_r.at[x], at_x(0), x > 0)

    arrive(xin.at[0], px_r.at[4])
    arrive(xin.at[3], px_r.at[3])
    arrive(xin.at[1], px_r.at[5])
    arrive(xin.at[2], px_r.at[2])
    for half in (0, 1):
        both = slice(2 * half, 2 * half + 2)
        s2x[both] = (ptb[both, x].astype(F32) + xin[half].astype(F32) + xin[3 - half].astype(F32)).astype(BF)
    for o in (2, 1, 3):
        send(s2x.at[:, :, lanes(ypeer(o))], r2y.at[o - 1], p2_s.at[o - 1], p2_r.at[o - 1], at_y(ypeer(o)))
    arrive(yin.at[0], py_r.at[4])
    arrive(yin.at[3], py_r.at[3])
    arrive(yin.at[1], py_r.at[5])
    arrive(yin.at[2], py_r.at[2])
    for half in (0, 1):
        both, here = slice(4 + 2 * half, 6 + 2 * half), slice(2 * half, 2 * half + 2)
        s2y[here] = (ptb[both, :, :, lanes(y)].astype(F32) + yin[half].astype(F32) + yin[3 - half].astype(F32)).astype(BF)
    for o in (2, 1, 3):
        send(s2y.at[:, xpeer(o)], r2x.at[o - 1], p2_s.at[o + 2], p2_r.at[o + 2], at_x(xpeer(o)))

    for o in range(1, NX):
        arrive(gk1.at[o - 1], gk1_r.at[o - 1])
    total = sgk[pl.ds(pl.multiple_of(x * 32, 32), 32), :].astype(F32)
    for o in range(1, NX):
        total += gk1[o - 1].astype(F32)
    gk1s[...] = total.astype(BF)
    send(gk1s, gk2.at[z], gk2_s, gk2_r.at[z], at_z(0), z > 0)

    @pl.when(col0)
    def _():
        for xx in range(1, NX):
            arrive(gv2.at[xx], gv2_r.at[xx])
        total = gv1s[...].astype(F32)
        for xx in range(1, NX):
            total += gv2[xx].astype(F32)
        gv2s[...] = total.astype(BF)

    send(gv2s, gv3.at[z], gv3_s, gv3_r.at[z], at_z(0), col0 & has_prev)

    def project(n, carry):
        proj_ref[:, lanes(n, 256)] = dot(attn_all[...], wfull[:, lanes(n, 256)], 1, 0).astype(BF)
        return carry

    lax.fori_loop(0, 4, project, 0)

    for o in range(1, NX):
        arrive(r2y.at[o - 1], p2_r.at[o - 1])
    total = s2x[:, :, lanes(y)].astype(F32)
    for o in range(1, NY):
        total += r2y[o - 1].astype(F32)
    red[0:4] = total.astype(BF)
    for o in range(1, NX):
        arrive(r2x.at[o - 1], p2_r.at[o + 2])
    total = s2y[:, x].astype(F32)
    for o in range(1, NX):
        total += r2x[o - 1].astype(F32)
    red[4:8] = total.astype(BF)
    for oz in (4, 5, 3, 6, 2, 7, 1):
        send(red.at[zpeer(oz)], r3.at[oz - 1], p3_s.at[oz - 1], p3_r.at[oz - 1], at_z(zpeer(oz)))
    send(pg.at[0], pg_recv.at[0], pg_s.at[0], pg_r.at[0], (c - 1, d), has_prev)

    @pl.when(row0)
    def _():
        for zz in range(1, NZ):
            arrive(gk2.at[zz], gk2_r.at[zz])
        total = gk1s[...].astype(F32)
        for zz in range(1, NZ):
            total += gk2[zz].astype(F32)
        gk2s[...] = total.astype(BF)

    send(gk2s, gk3.at[x], gk3_s, gk3_r.at[x], at_x(0), row0 & has_prev)

    lax.fori_loop(4, 8, project, 0)

    for n, out_ref in ((1, dv_ref), (0, dk_ref)):
        arrive(pg_recv.at[n], pg_r.at[n], has_next)
        out_ref[0:BLK] = acc[n, 0:BLK].astype(BF)

        @pl.when(has_next)
        def _(n=n, out_ref=out_ref):
            out_ref[BLK:] = (acc[n, BLK:] + pg_recv[n].astype(F32)).astype(BF)

        @pl.when(jnp.logical_not(has_next))
        def _(n=n, out_ref=out_ref):
            out_ref[BLK:] = acc[n, BLK:].astype(BF)

    for oz in range(1, NZ):
        arrive(r3.at[oz - 1], p3_r.at[oz - 1])
    total = red[z].astype(F32)
    for oz in range(1, NZ):
        total += r3[oz - 1].astype(F32)
    gp_ref[...] = total * (1.0 / 256.0)

    @pl.when(root)
    def _():
        for zz in range(1, NZ):
            arrive(gv3.at[zz], gv3_r.at[zz])
        for zz in range(NZ):
            rows = slice(16 * zz, 16 * zz + 16)
            part = gv2s[...] if zz == 0 else gv3[zz]
            dv_ref[rows] = (acc[1, rows] + part.astype(F32)).astype(BF)
        for xx in range(1, NX):
            arrive(gk3.at[xx], gk3_r.at[xx])
        for xx in range(NX):
            rows = slice(32 * xx, 32 * xx + 32)
            part = gk2s[...] if xx == 0 else gk3[xx]
            dk_ref[rows] = (acc[0, rows] + part.astype(F32)).astype(BF)

    for cond, copy in pending:
        if cond is None:
            copy.wait_send()
        else:
            pl.when(cond)(lambda copy=copy: copy.wait_send())


def store(*refs):
    count = (len(refs) - 1) // 2
    copies = [pltpu.make_async_copy(refs[n], refs[count + n], refs[-1].at[n]) for n in range(count)]
    for copy in copies:
        copy.start()
    for copy in copies:
        copy.wait()


def body(queries, keys, values, cotangent, proj_weight, pattern):
    rows, width = queries.shape[1:]
    full = cotangent.shape[2]
    vmem, hbm = pl.BlockSpec(memory_space=pltpu.VMEM), pl.BlockSpec(memory_space=pltpu.HBM)
    V, D = pltpu.VMEM, pltpu.SemaphoreType.DMA
    scratch = [
        V((HEADS, 2, 64), jnp.int32), V((rows, width), BF), V((rows, full), BF),
        V((1024, full), BF), V((2, 512, width), BF), V((full, 512), BF), V((rows, full), BF),
        V((512, 512), BF), V((rows, 512), BF), V((rows, width), BF), V((rows, width), BF),
        V((2, HEADS, 4 * BLK), F32), V((256, 512), F32), V((HEADS, 256, 512), F32),
        V((2, 256, width), F32), V((2, 128, width), BF), V((2, 128, width), BF),
        V((128, width), BF), V((3, 32, width), BF), V((32, width), BF), V((8, 32, width), BF), V((32, width), BF), V((4, 32, width), BF),
        V((128, width), BF), V((7, 16, width), BF), V((16, width), BF), V((4, 16, width), BF), V((16, width), BF), V((8, 16, width), BF),
        V((8, 4, 64, 512), BF),
        V((2, 2, 64, 512), BF), V((2, 2, 64, 512), BF), V((4, 2, 64, 512), BF),
        V((2, 2, 4, 64, 128), BF), V((2, 2, 4, 64, 128), BF), V((4, 2, 4, 64, 128), BF),
        V((4, 64, 512), BF), V((4, 4, 64, 128), BF), V((3, 4, 64, 128), BF), V((3, 4, 64, 128), BF),
        V((8, 64, 128), BF), V((7, 64, 128), BF),
        D((8,)), D((3,)), D((2,)), D((3, 2)), D((3, 2)), D((6,)), D((6,)), D((11,)), D((4,)), D((28,)), D((7,)), D((6,)), D((3,)),
        D((20,)), D((7,)),
        D((2,)), D((2,)), D((3,)), D((3,)), D, D((8,)), D, D((4,)), D((7,)), D((7,)), D, D((4,)), D, D((8,)),
        D((6,)), D((6,)), D((6,)), D((6,)), D((6,)), D((6,)), D((7,)), D((7,)),
    ]
    shapes = [((rows, full), BF), ((rows, width), BF), ((rows, width), BF), ((rows, width), BF), ((64, 128), F32)]
    outs = pl.pallas_call(
        kernel,
        out_shape=[pltpu.VMEM(*s) for s in shapes],
        in_specs=[hbm] * 6,
        out_specs=[vmem] * 5,
        scratch_shapes=scratch,
        compiler_params=pltpu.CompilerParams(
            collective_id=0, has_side_effects=True, vmem_limit_bytes=58 * 1024 * 1024
        ),
        cost_estimate=pl.CostEstimate(flops=4_400_000_000, bytes_accessed=6_500_000, transcendentals=1_000_000),
    )(jnp.swapaxes(pattern, 2, 3)[0], queries[0], keys[0], values[0], cotangent[0], proj_weight)
    proj, dq, dk, dv, gp = pl.pallas_call(
        store,
        out_shape=[jax.ShapeDtypeStruct(*s) for s in shapes],
        in_specs=[pl.BlockSpec(memory_space=pl.ANY)] * 5,
        out_specs=[hbm] * 5,
        scratch_shapes=[D((5,))],
        compiler_params=pltpu.CompilerParams(vmem_limit_bytes=1024 * 1024),
    )(*outs)
    return proj[None], dq[None], dk[None], dv[None], gp.T


def solution(mesh):
    return jax.shard_map(
        body,
        mesh=mesh,
        in_specs=(
            P("dp", "ctx", None),
            P("dp", "ctx", None),
            P("dp", "ctx", None),
            P("dp", "ctx", None),
            P("dp", None),
            P("dp", None, None, None),
        ),
        out_specs=(
            P("dp", "ctx", None),
            P("dp", "ctx", None),
            P("dp", "ctx", None),
            P("dp", "ctx", None),
            P("dp", "ctx"),
        ),
        check_vma=False,
    )
```

```python
import jax
import jax.numpy as jnp
from jax import lax
from jax.experimental import pallas as pl
from jax.experimental.pallas import tpu as pltpu
from jax.sharding import PartitionSpec as P

MESH = pl.DeviceIdType.MESH
NX, NY, NZ = 4, 4, 8
HEADS, HDIM, BLK = 8, 128, 128
BF, F32 = jnp.bfloat16, jnp.float32
MASKED = -1.0e30
UNROLL = 4
SCALE = HDIM ** -0.5
SCALE2 = SCALE * 1.4426950408889634


def lanes(index, size=128):
    return pl.ds(pl.multiple_of(index * size, size), size)


def dot(a, b, da, db):
    return lax.dot_general(a, b, (((da,), (db,)), ((), ())), preferred_element_type=F32)


def kernel(pat_ref, q_ref, k_ref, v_ref, cot_ref, w_ref,
           proj_ref, dq_ref, dk_ref, dv_ref, gp_ref,
           pat, q, cot, wfull, kv, ct, cot_peer, a2, attn_send, attn_all, grad, gate, bias, probs,
           acc, pg, pg_recv, sgk, gk1, gk1s, gk2, gk2s, gk3, sgv, gv1, gv1s, gv2, gv2s, gv3,
           ptb, xfwd, xmrg, xin, yfwd, ymrg, yin, s2x, s2y, r2x, r2y, red, r3,
           local, prev_s, prev_r, w_s, w_r, core_s, core_r, sk_s, sk_r, kz_s, kz_r, kx_s, kx_r, vz_s, vz_r,
           pg_s, pg_r, gk1_s, gk1_r, gk2_s, gk2_r, gk3_s, gk3_r, gv1_s, gv1_r, gv2_s, gv2_r, gv3_s, gv3_r,
           px_s, px_r, py_s, py_r, p2_s, p2_r, p3_s, p3_r):
    c = lax.axis_index("ctx")
    d = lax.axis_index("dp")
    x, z = lax.rem(c, NX), lax.div(c, NX)
    y, core = lax.div(d, 2), lax.rem(d, 2)

    def xpeer(o):
        return lax.rem(x + o, NX)

    def ypeer(o):
        return lax.rem(y + o, NY)

    def zpeer(o):
        return lax.rem(z + o, NZ)

    def at_x(xx):
        return (z * NX + xx, d)

    def at_z(zz):
        return (zz * NX + x, d)

    def at_y(yy):
        return (c, yy * 2 + core)

    other = 1 - core
    at_core = (c, y * 2 + other)
    has_next, has_prev = c < NX * NZ - 1, c > 0
    root, row0, col0 = c == 0, z == 0, x == 0
    pending = []

    def remote(src, dst, send, recv, device):
        return pltpu.make_async_remote_copy(src_ref=src, dst_ref=dst, send_sem=send, recv_sem=recv,
                                            device_id=device, device_id_type=MESH)

    def send(src, dst, send_sem, recv_sem, device, cond=None):
        copy = remote(src, dst, send_sem, recv_sem, device)
        pending.append((cond, copy))
        if cond is None:
            copy.start()
        else:
            pl.when(cond)(lambda: copy.start())

    def arrive(dst, recv_sem, cond=None):
        copy = remote(dst, dst, recv_sem, recv_sem, at_core)
        if cond is None:
            copy.wait_recv()
        else:
            pl.when(cond)(lambda: copy.wait_recv())

    def drain(count):
        for cond, copy in pending[:count]:
            if cond is None:
                copy.wait_send()
            else:
                pl.when(cond)(lambda copy=copy: copy.wait_send())
        del pending[:count]

    own = pl.ds(2 * BLK, 2 * BLK)
    loads = [
        pltpu.make_async_copy(k_ref, kv.at[0, own], local.at[0]),
        pltpu.make_async_copy(v_ref, kv.at[1, own], local.at[1]),
        pltpu.make_async_copy(w_ref, wfull.at[lanes(d)], local.at[2]),
        pltpu.make_async_copy(cot_ref, cot, local.at[3]),
        pltpu.make_async_copy(q_ref, q, local.at[4]),
        pltpu.make_async_copy(pat_ref, pat, local.at[5]),
    ]
    for load in loads:
        load.start()
    sink_loads = [
        pltpu.make_async_copy(k_ref.at[pl.ds(0, BLK)], kv.at[0, pl.ds(0, BLK)], local.at[6]),
        pltpu.make_async_copy(v_ref.at[pl.ds(0, BLK)], kv.at[1, pl.ds(0, BLK)], local.at[7]),
    ]
    for load in sink_loads:
        pl.when(root)(lambda load=load: load.start())

    barrier = pltpu.get_barrier_semaphore()

    def greet(device):
        pl.semaphore_signal(barrier, inc=1, device_id=device, device_id_type=MESH)

    for o in range(1, NZ):
        greet(at_z(zpeer(o)))
    for o in range(1, NX):
        greet(at_x(xpeer(o)))
    for o in range(1, NY):
        greet(at_y(ypeer(o)))
    greet(at_core)
    far_next = (x == NX - 1) & has_next
    far_prev = col0 & has_prev
    pl.when(far_next)(lambda: greet((c + 1, d)))
    pl.when(far_prev)(lambda: greet((c - 1, d)))
    pl.semaphore_wait(barrier, NX + NY + NZ - 2 + far_next.astype(jnp.int32) + far_prev.astype(jnp.int32))

    def krows(ref, xx):
        return ref.at[pl.ds(pl.multiple_of(xx * 32, 32), 32)]

    def vrows(ref, zz):
        return ref.at[pl.ds(pl.multiple_of(zz * 16, 16), 16)]

    skeys, svalues = kv.at[0], kv.at[1]

    def kchunk(xx, zz):
        return skeys.at[pl.ds(pl.multiple_of(xx * 32, 32), 32), lanes(zz)]

    for o in (2, 1, 3):
        send(k_ref.at[pl.ds(o * 32, 32)], skeys.at[pl.ds(o * 32, 32)], sk_s.at[o], sk_r.at[0], at_x(o), root)
    for o in (4, 5, 3, 6, 2, 7, 1):
        send(v_ref.at[pl.ds(o * 16, 16)], svalues.at[pl.ds(o * 16, 16)], sk_s.at[3 + o], sk_r.at[1], at_z(o), root)

    def wrows(dd, half):
        return wfull.at[pl.ds(pl.multiple_of(dd * 128 + half * 64, 64), 64)]

    up, down, opposite = ypeer(1), ypeer(3), ypeer(2)
    for way, half in ((0, 0), (1, 1), (0, 1), (1, 0)):
        send(w_ref.at[pl.ds(half * 64, 64)], wrows(d, half), w_s.at[way, half], w_r.at[way, half], at_y((up, down)[way]))
    send(k_ref.at[pl.ds(BLK, BLK)], kv.at[0, pl.ds(BLK, BLK)], prev_s.at[0], prev_r.at[0], (c + 1, d), has_next & (z > 0))
    send(cot_ref, cot_peer, core_s.at[1], core_r.at[1], at_core)
    send(w_ref, wfull.at[lanes(d)], core_s.at[0], core_r.at[0], at_core)

    arrive(krows(skeys, x), sk_r.at[0], row0 & has_prev)
    for oz in (4, 5, 3, 6, 2, 7, 1):
        send(skeys.at[pl.ds(pl.multiple_of(x * 32, 32), 32), pl.ds(oz * 128, 128)],
             kchunk(x, oz), kz_s.at[6 + oz], sk_r.at[2], at_z(oz), row0 & has_prev)
        send(k_ref.at[pl.ds(0, 32), pl.ds(oz * 128, 128)], kchunk(0, oz), kz_s.at[13 + oz], sk_r.at[2], at_z(oz), root)
    send(k_ref.at[pl.ds(BLK, BLK)], kv.at[0, pl.ds(BLK, BLK)], prev_s.at[2], prev_r.at[0], (c + 1, d), row0)
    arrive(kchunk(x, z), sk_r.at[2], z > 0)
    for oz in (4, 5, 3, 6, 2, 7, 1):
        send(kchunk(x, z), kchunk(x, z), kz_s.at[oz - 1], kz_r.at[oz - 1], at_z(zpeer(oz)), (zpeer(oz) > 0) & has_prev)
        send(k_ref.at[pl.ds(0, 32), pl.ds(0, 128)], kchunk(0, 0), kz_s.at[20 + oz], kz_r.at[oz - 1], at_z(oz), root)
    arrive(vrows(svalues, z), sk_r.at[1], col0 & has_prev)
    for o in (2, 1, 3):
        send(vrows(svalues, z), vrows(svalues, z), vz_s.at[6 + o], sk_r.at[3], at_x(o), col0 & has_prev)
        send(v_ref.at[pl.ds(0, 16)], svalues.at[pl.ds(0, 16)], vz_s.at[9 + o], sk_r.at[3], at_x(o), root)

    arrive(vrows(svalues, z), sk_r.at[3], x > 0)
    send(v_ref.at[pl.ds(BLK, BLK)], kv.at[1, pl.ds(BLK, BLK)], prev_s.at[1], prev_r.at[1], (c + 1, d), has_next)

    for oz in (4, 5, 3, 6, 2, 7, 1):
        send(vrows(svalues, z), vrows(svalues, z), vz_s.at[oz - 1], vz_r.at[oz - 1], at_z(zpeer(oz)),
             has_prev & ((x > 0) | (zpeer(oz) > 0)))
        send(v_ref.at[pl.ds(0, 16)], svalues.at[pl.ds(0, 16)], vz_s.at[12 + oz], vz_r.at[oz - 1], at_z(oz), root)

    for load in loads:
        load.wait()
    for load in sink_loads:
        pl.when(root)(lambda load=load: load.wait())

    @pl.when(root)
    def _():
        kv[0, BLK:2 * BLK] = jnp.zeros((BLK, HEADS * HDIM), BF)
        kv[1, BLK:2 * BLK] = jnp.zeros((BLK, HEADS * HDIM), BF)

    row = lax.broadcasted_iota(jnp.int32, (2 * BLK, 4 * BLK), 0)
    col = lax.broadcasted_iota(jnp.int32, (2 * BLK, 4 * BLK), 1)
    inside = lax.rem(col, BLK) <= lax.rem(row, BLK)
    col_blk, row_blk = lax.div(col, BLK), lax.div(row, BLK)
    first_shard = jnp.full((2 * BLK, 4 * BLK), c, jnp.int32) == 0
    keep = ((col_blk == 0) & (~first_shard | (row_blk == 1) | inside)) \
        | ((col_blk == 2) & (row_blk == 0) & inside & ~first_shard) \
        | ((col_blk == 3) & (row_blk == 1) & inside) \
        | (col_blk == row_blk + 1)
    bias[...] = jnp.where(keep, 0.0, MASKED)
    reach = pat[:, 1, :]
    block = lax.broadcasted_iota(jnp.int32, reach.shape, 1)
    for n in (0, 1):
        hit = (block == 2 * c + n) & (reach == 1) & (jnp.full(reach.shape, c, jnp.int32) > 0)
        on = jnp.max(jnp.where(hit, 1.0, 0.0), axis=1, keepdims=True)
        gate[n] = jnp.zeros((HEADS, 4 * BLK), F32)
        gate[n, :, (n + 1) * BLK:(n + 2) * BLK] = jnp.broadcast_to(jnp.where(on > 0.5, 0.0, MASKED), (HEADS, BLK))

    d_down, d_up, d_opp = down * 2 + core, up * 2 + core, opposite * 2 + core
    arrive(wrows(d_down, 0), w_r.at[0, 0])
    send(wrows(d_down, 0), wrows(d_down, 0), w_s.at[2, 0], w_r.at[2, 0], at_y(up))
    arrive(wrows(d_up, 1), w_r.at[1, 1])
    send(wrows(d_up, 1), wrows(d_up, 1), w_s.at[2, 1], w_r.at[2, 1], at_y(down))

    for oz in range(1, NZ):
        arrive(kchunk(x, zpeer(NZ - oz)), kz_r.at[oz - 1], z > 0)
    for o in (2, 1, 3):
        send(krows(skeys, x), krows(skeys, x), kx_s.at[o - 1], kx_r.at[o - 1], at_x(xpeer(o)), has_prev & ((z > 0) | (xpeer(o) > 0)))
        send(k_ref.at[pl.ds(0, 32)], skeys.at[pl.ds(0, 32)], kx_s.at[2 + o], kx_r.at[o - 1], at_x(o), root)

    def turn(n, carry):
        ct[lanes(n, 256), 0:256] = cot[:, lanes(n, 256)].T
        return carry

    lax.fori_loop(0, 8, turn, 0)

    arrive(wrows(d_down, 1), w_r.at[0, 1])
    send(wfull.at[lanes(d_down)], wfull.at[lanes(d_down)], core_s.at[2], core_r.at[2], at_core)
    arrive(wrows(d_up, 0), w_r.at[1, 0])
    send(wfull.at[lanes(d_up)], wfull.at[lanes(d_up)], core_s.at[3], core_r.at[3], at_core)

    arrive(cot_peer, core_r.at[1])

    def turn_peer(n, carry):
        ct[lanes(n, 256), 256:512] = cot_peer[:, lanes(n, 256)].T
        return carry

    lax.fori_loop(0, 8, turn_peer, 0)

    for o in range(1, NX):
        arrive(krows(skeys, xpeer(NX - o)), kx_r.at[o - 1], has_prev)
    for oz in range(1, NZ):
        arrive(vrows(svalues, zpeer(NZ - oz)), vz_r.at[oz - 1], has_prev)
    arrive(kv.at[0, pl.ds(BLK, BLK)], prev_r.at[0], has_prev)
    arrive(kv.at[1, pl.ds(BLK, BLK)], prev_r.at[1], has_prev)

    def forward(h):
        cols = lanes(h)
        s = dot(q[:, cols], kv[0, :, cols], 1, 1) * SCALE2 + bias[...]
        s = jnp.concatenate([s[0:BLK] + gate[0, pl.ds(h, 1), :], s[BLK:] + gate[1, pl.ds(h, 1), :]], axis=0)
        e = jnp.exp2(s - jnp.max(s, axis=1, keepdims=True))
        p = e * (1.0 / jnp.sum(e, axis=1, keepdims=True))
        return p, dot(p.astype(BF), kv[1, :, cols], 1, 0).astype(BF)

    def forward_some(j, parity):
        heads = [2 * (UNROLL * j + n) + parity for n in range(UNROLL)]
        done = [forward(h) for h in heads]
        for n, (p, out) in enumerate(done):
            probs[heads[n]] = p
            attn_all[:, lanes(heads[n])] = out
        return [(lanes(UNROLL * j + n), out) for n, (_, out) in enumerate(done)]

    def forward_other(j, carry):
        for place, out in forward_some(j, other):
            attn_send[:, place] = out
        return carry

    def forward_own(j, carry):
        for place, out in forward_some(j, core):
            a2[0:256, place] = out
        return carry

    lax.fori_loop(0, 4 // UNROLL, forward_other, 0)
    send(attn_send, a2.at[pl.ds(256, 256)], core_s.at[4], core_r.at[4], at_core)
    arrive(wrows(d_opp, 0), w_r.at[2, 0])
    arrive(wrows(d_opp, 1), w_r.at[2, 1])
    send(wfull.at[lanes(d_opp)], wfull.at[lanes(d_opp)], core_s.at[5], core_r.at[5], at_core)
    lax.fori_loop(0, 4 // UNROLL, forward_own, 0)

    arrive(a2.at[pl.ds(256, 256)], core_r.at[4])

    def partial(zz, carry):
        ptb[zz] = dot(ct[lanes(zz, 256), :], a2[...], 1, 0).astype(BF).reshape(NX, 64, 512)
        return carry

    xu, xd, xo = xpeer(1), xpeer(3), xpeer(2)

    def xpart(lo, xx):
        return ptb.at[pl.ds(lo, 2), xx]

    def ypart(lo, yy):
        return ptb.at[pl.ds(lo, 2), :, :, lanes(yy)]

    lax.fori_loop(0, 4, partial, 0)
    send(xpart(0, xo), xfwd.at[0], px_s.at[0], px_r.at[0], at_x(xu))
    send(xpart(2, xo), xfwd.at[1], px_s.at[1], px_r.at[1], at_x(xd))
    send(xpart(2, xu), xin.at[2], px_s.at[2], px_r.at[2], at_x(xu))
    send(xpart(0, xd), xin.at[3], px_s.at[3], px_r.at[3], at_x(xd))
    lax.fori_loop(4, 8, partial, 0)
    send(ypart(4, opposite), yfwd.at[0], py_s.at[0], py_r.at[0], at_y(up))
    send(ypart(6, opposite), yfwd.at[1], py_s.at[1], py_r.at[1], at_y(down))
    send(ypart(6, up), yin.at[2], py_s.at[2], py_r.at[2], at_y(up))
    send(ypart(4, down), yin.at[3], py_s.at[3], py_r.at[3], at_y(down))

    def peer_rows(dd):
        return wfull.at[lanes(dd)]

    arrive(peer_rows(y * 2 + other), core_r.at[0])
    arrive(peer_rows(down * 2 + other), core_r.at[2])
    arrive(peer_rows(up * 2 + other), core_r.at[3])
    arrive(peer_rows(opposite * 2 + other), core_r.at[5])

    def grad_attn(n, carry):
        grad[:, lanes(n, 256)] = dot(cot[...], wfull[lanes(n, 256), :], 1, 1).astype(BF)
        return carry

    lax.fori_loop(0, 4, grad_attn, 0)

    def backward_values(j, carry):
        places = [lanes(UNROLL * j + n) for n in range(UNROLL)]
        terms = [dot(probs[UNROLL * j + n].astype(BF), grad[:, cols], 0, 0) for n, cols in enumerate(places)]
        for cols, term in zip(places, terms):
            sgv[:, cols] = term[0:128].astype(BF)
            pg[1, :, cols] = term[128:256].astype(BF)
            acc[1, :, cols] = term[256:512]
        return carry

    lax.fori_loop(0, HEADS // UNROLL, backward_values, 0)
    for oz in (4, 5, 3, 6, 2, 7, 1):
        send(vrows(sgv, zpeer(oz)), gv1.at[oz - 1], gv1_s.at[oz - 1], gv1_r.at[oz - 1], at_z(zpeer(oz)))

    def merge(fwd, part):
        return (fwd.astype(F32) + part.astype(F32)).astype(BF)

    arrive(xfwd.at[0], px_r.at[0])
    xmrg[0] = merge(xfwd[0], ptb[0:2, xu])
    send(xmrg.at[0], xin.at[0], px_s.at[4], px_r.at[4], at_x(xu))
    arrive(xfwd.at[1], px_r.at[1])
    xmrg[1] = merge(xfwd[1], ptb[2:4, xd])
    send(xmrg.at[1], xin.at[1], px_s.at[5], px_r.at[5], at_x(xd))
    arrive(yfwd.at[0], py_r.at[0])
    ymrg[0] = merge(yfwd[0], ptb[4:6, :, :, lanes(up)])
    send(ymrg.at[0], yin.at[0], py_s.at[4], py_r.at[4], at_y(up))
    arrive(yfwd.at[1], py_r.at[1])
    ymrg[1] = merge(yfwd[1], ptb[6:8, :, :, lanes(down)])
    send(ymrg.at[1], yin.at[1], py_s.at[5], py_r.at[5], at_y(down))
    send(pg.at[1], pg_recv.at[1], pg_s.at[1], pg_r.at[1], (c - 1, d), has_prev)

    sent_early = len(pending)

    def backward_head(h):
        cols = lanes(h)
        g = grad[:, cols]
        delta = jnp.sum(g.astype(F32) * attn_all[:, cols].astype(F32), axis=1, keepdims=True)
        ds = (probs[h] * (dot(g, kv[1, :, cols], 1, 1) - delta)).astype(BF)
        return cols, dot(ds, q[:, cols], 0, 0) * SCALE, (dot(ds, kv[0, :, cols], 1, 0) * SCALE).astype(BF)

    def backward(j, carry):
        for cols, term, query_grad in [backward_head(UNROLL * j + n) for n in range(UNROLL)]:
            sgk[:, cols] = term[0:128].astype(BF)
            pg[0, :, cols] = term[128:256].astype(BF)
            acc[0, :, cols] = term[256:512]
            dq_ref[:, cols] = query_grad
        return carry

    lax.fori_loop(0, HEADS // UNROLL, backward, 0)
    for o in (2, 1, 3):
        send(krows(sgk, xpeer(o)), gk1.at[o - 1], gk1_s.at[o - 1], gk1_r.at[o - 1], at_x(xpeer(o)))

    for oz in range(1, NZ):
        arrive(gv1.at[oz - 1], gv1_r.at[oz - 1])
    total = sgv[pl.ds(pl.multiple_of(z * 16, 16), 16), :].astype(F32)
    for oz in range(1, NZ):
        total += gv1[oz - 1].astype(F32)
    gv1s[...] = total.astype(BF)
    send(gv1s, gv2.at[x], gv2_s, gv2_r.at[x], at_x(0), x > 0)

    arrive(yin.at[0], py_r.at[4])
    arrive(yin.at[3], py_r.at[3])
    arrive(yin.at[1], py_r.at[5])
    arrive(yin.at[2], py_r.at[2])
    for half in (0, 1):
        both, here = slice(4 + 2 * half, 6 + 2 * half), slice(2 * half, 2 * half + 2)
        s2y[here] = (ptb[both, :, :, lanes(y)].astype(F32) + yin[half].astype(F32) + yin[3 - half].astype(F32)).astype(BF)
    for o in (2, 1, 3):
        send(s2y.at[:, xpeer(o)], r2x.at[o - 1], p2_s.at[o + 2], p2_r.at[o + 2], at_x(xpeer(o)))

    arrive(xin.at[0], px_r.at[4])
    arrive(xin.at[3], px_r.at[3])
    arrive(xin.at[1], px_r.at[5])
    arrive(xin.at[2], px_r.at[2])
    for half in (0, 1):
        both = slice(2 * half, 2 * half + 2)
        s2x[both] = (ptb[both, x].astype(F32) + xin[half].astype(F32) + xin[3 - half].astype(F32)).astype(BF)
    for o in (2, 1, 3):
        send(s2x.at[:, :, lanes(ypeer(o))], r2y.at[o - 1], p2_s.at[o - 1], p2_r.at[o - 1], at_y(ypeer(o)))

    for o in range(1, NX):
        arrive(gk1.at[o - 1], gk1_r.at[o - 1])
    total = sgk[pl.ds(pl.multiple_of(x * 32, 32), 32), :].astype(F32)
    for o in range(1, NX):
        total += gk1[o - 1].astype(F32)
    gk1s[...] = total.astype(BF)
    send(gk1s, gk2.at[z], gk2_s, gk2_r.at[z], at_z(0), z > 0)

    @pl.when(col0)
    def _():
        for xx in range(1, NX):
            arrive(gv2.at[xx], gv2_r.at[xx])
        total = gv1s[...].astype(F32)
        for xx in range(1, NX):
            total += gv2[xx].astype(F32)
        gv2s[...] = total.astype(BF)

    send(gv2s, gv3.at[z], gv3_s, gv3_r.at[z], at_z(0), col0 & has_prev)

    def project(n, carry):
        proj_ref[:, lanes(n, 256)] = dot(attn_all[...], wfull[:, lanes(n, 256)], 1, 0).astype(BF)
        return carry

    lax.fori_loop(0, 4, project, 0)

    drain(sent_early)

    for o in range(1, NX):
        arrive(r2y.at[o - 1], p2_r.at[o - 1])
    total = s2x[:, :, lanes(y)].astype(F32)
    for o in range(1, NY):
        total += r2y[o - 1].astype(F32)
    red[0:4] = total.astype(BF)
    for o in range(1, NX):
        arrive(r2x.at[o - 1], p2_r.at[o + 2])
    total = s2y[:, x].astype(F32)
    for o in range(1, NX):
        total += r2x[o - 1].astype(F32)
    red[4:8] = total.astype(BF)
    for oz in (4, 5, 3, 6, 2, 7, 1):
        send(red.at[zpeer(oz)], r3.at[oz - 1], p3_s.at[oz - 1], p3_r.at[oz - 1], at_z(zpeer(oz)))
    send(pg.at[0], pg_recv.at[0], pg_s.at[0], pg_r.at[0], (c - 1, d), has_prev)

    @pl.when(row0)
    def _():
        for zz in range(1, NZ):
            arrive(gk2.at[zz], gk2_r.at[zz])
        total = gk1s[...].astype(F32)
        for zz in range(1, NZ):
            total += gk2[zz].astype(F32)
        gk2s[...] = total.astype(BF)

    send(gk2s, gk3.at[x], gk3_s, gk3_r.at[x], at_x(0), row0 & has_prev)

    lax.fori_loop(4, 8, project, 0)

    for oz in range(1, NZ):
        arrive(r3.at[oz - 1], p3_r.at[oz - 1])
    total = red[z].astype(F32)
    for oz in range(1, NZ):
        total += r3[oz - 1].astype(F32)
    gp_ref[...] = total * (1.0 / 256.0)

    for n, out_ref in ((1, dv_ref), (0, dk_ref)):
        arrive(pg_recv.at[n], pg_r.at[n], has_next)
        out_ref[0:BLK] = acc[n, 0:BLK].astype(BF)

        @pl.when(has_next)
        def _(n=n, out_ref=out_ref):
            out_ref[BLK:] = (acc[n, BLK:] + pg_recv[n].astype(F32)).astype(BF)

        @pl.when(jnp.logical_not(has_next))
        def _(n=n, out_ref=out_ref):
            out_ref[BLK:] = acc[n, BLK:].astype(BF)

    @pl.when(root)
    def _():
        for zz in range(1, NZ):
            arrive(gv3.at[zz], gv3_r.at[zz])
        for zz in range(NZ):
            rows = slice(16 * zz, 16 * zz + 16)
            part = gv2s[...] if zz == 0 else gv3[zz]
            dv_ref[rows] = (acc[1, rows] + part.astype(F32)).astype(BF)
        for xx in range(1, NX):
            arrive(gk3.at[xx], gk3_r.at[xx])
        for xx in range(NX):
            rows = slice(32 * xx, 32 * xx + 32)
            part = gk2s[...] if xx == 0 else gk3[xx]
            dk_ref[rows] = (acc[0, rows] + part.astype(F32)).astype(BF)

    drain(len(pending))


def store(*refs):
    count = (len(refs) - 1) // 2
    copies = [pltpu.make_async_copy(refs[n], refs[count + n], refs[-1].at[n]) for n in range(count)]
    for copy in copies:
        copy.start()
    for copy in copies:
        copy.wait()


def body(queries, keys, values, cotangent, proj_weight, pattern):
    rows, width = queries.shape[1:]
    full = cotangent.shape[2]
    vmem, hbm = pl.BlockSpec(memory_space=pltpu.VMEM), pl.BlockSpec(memory_space=pltpu.HBM)
    V, D = pltpu.VMEM, pltpu.SemaphoreType.DMA
    scratch = [
        V((HEADS, 2, 64), jnp.int32), V((rows, width), BF), V((rows, full), BF),
        V((1024, full), BF), V((2, 512, width), BF), V((full, 512), BF), V((rows, full), BF),
        V((512, 512), BF), V((rows, 512), BF), V((rows, width), BF), V((rows, width), BF),
        V((2, HEADS, 4 * BLK), F32), V((256, 512), F32), V((HEADS, 256, 512), F32),
        V((2, 256, width), F32), V((2, 128, width), BF), V((2, 128, width), BF),
        V((128, width), BF), V((3, 32, width), BF), V((32, width), BF), V((8, 32, width), BF), V((32, width), BF), V((4, 32, width), BF),
        V((128, width), BF), V((7, 16, width), BF), V((16, width), BF), V((4, 16, width), BF), V((16, width), BF), V((8, 16, width), BF),
        V((8, 4, 64, 512), BF),
        V((2, 2, 64, 512), BF), V((2, 2, 64, 512), BF), V((4, 2, 64, 512), BF),
        V((2, 2, 4, 64, 128), BF), V((2, 2, 4, 64, 128), BF), V((4, 2, 4, 64, 128), BF),
        V((4, 64, 512), BF), V((4, 4, 64, 128), BF), V((3, 4, 64, 128), BF), V((3, 4, 64, 128), BF),
        V((8, 64, 128), BF), V((7, 64, 128), BF),
        D((8,)), D((3,)), D((2,)), D((3, 2)), D((3, 2)), D((6,)), D((6,)), D((11,)), D((4,)), D((28,)), D((7,)), D((6,)), D((3,)),
        D((20,)), D((7,)),
        D((2,)), D((2,)), D((3,)), D((3,)), D, D((8,)), D, D((4,)), D((7,)), D((7,)), D, D((4,)), D, D((8,)),
        D((6,)), D((6,)), D((6,)), D((6,)), D((6,)), D((6,)), D((7,)), D((7,)),
    ]
    shapes = [((rows, full), BF), ((rows, width), BF), ((rows, width), BF), ((rows, width), BF), ((64, 128), F32)]
    outs = pl.pallas_call(
        kernel,
        out_shape=[pltpu.VMEM(*s) for s in shapes],
        in_specs=[hbm] * 6,
        out_specs=[vmem] * 5,
        scratch_shapes=scratch,
        compiler_params=pltpu.CompilerParams(
            collective_id=0, has_side_effects=True, vmem_limit_bytes=58 * 1024 * 1024
        ),
        cost_estimate=pl.CostEstimate(flops=4_400_000_000, bytes_accessed=6_500_000, transcendentals=1_000_000),
    )(jnp.swapaxes(pattern, 2, 3)[0], queries[0], keys[0], values[0], cotangent[0], proj_weight)
    proj, dq, dk, dv, gp = pl.pallas_call(
        store,
        out_shape=[jax.ShapeDtypeStruct(*s) for s in shapes],
        in_specs=[pl.BlockSpec(memory_space=pl.ANY)] * 5,
        out_specs=[hbm] * 5,
        scratch_shapes=[D((5,))],
        compiler_params=pltpu.CompilerParams(vmem_limit_bytes=1024 * 1024),
    )(*outs)
    return proj[None], dq[None], dk[None], dv[None], gp.T


def solution(mesh):
    return jax.shard_map(
        body,
        mesh=mesh,
        in_specs=(
            P("dp", "ctx", None),
            P("dp", "ctx", None),
            P("dp", "ctx", None),
            P("dp", "ctx", None),
            P("dp", None),
            P("dp", None, None, None),
        ),
        out_specs=(
            P("dp", "ctx", None),
            P("dp", "ctx", None),
            P("dp", "ctx", None),
            P("dp", "ctx", None),
            P("dp", "ctx"),
        ),
        check_vma=False,
    )
```
